32 devices in a mesh: group: 2 (over y), ep: 4 (over z), tp: 2 (over x), dp: 2 (over core).
Axes of the slice: x: 2, y: 2, z: 4, core: 2. Of those that a mesh axis runs over, the one named last changes fastest.
Arguments:
- tokens: bfloat16 [128, 6144], P(('group', 'ep', 'dp')), parts along dimension 0, may hold values from -70 to 70
- norm_gain: float32 [6144], P('tp'), may hold values from 0.5 to 1.5
- expert_ids: int32 [128, 4], P(('group', 'ep', 'dp')), parts along dimension 0, may hold values from 0 to 7, all different within a row; in each aligned block of 8 rows (0 to 7, 8 to 15, ...) at most 5 rows name the same one
- route_weight: float32 [128, 4], P(('group', 'ep', 'dp')), parts along dimension 0, may hold values from 0.05 to 1
- w_up: bfloat16 [6144, 49152], P(None, ('ep', 'tp', 'dp')), may hold values from -0.078125 to 0.078125
- w_down: bfloat16 [49152, 6144], P(('ep', 'tp', 'dp')), may hold values from -0.15625 to 0.15625
- w_qkv: bfloat16 [6144, 4096], P('tp', ('ep', 'dp')), may hold values from -0.078125 to 0.078125
Outputs:
- qkv: bfloat16 [128, 4096], P(('group', 'tp'), ('ep', 'dp')), parts along dimension 0
The draws below stay inside these ranges and needn't reach their ends.
There are 2 independent parts, one for each index of `group`. The reference program is written for one: setup_inputs(seed, part) draws one part's arguments, and reference() takes and returns one part's arrays. A program takes and returns all parts, laid end to end along the dimension named above; an argument that names none is the same for every part. Nothing has to cross between parts.
Inputs may be any that keep to these rules, and one draw needn't show every extreme that they name: `expert_ids`: each row names 4 different experts. In each aligned block of 8 rows (the rows of one device) no expert is named by more than 5 rows, a bound that some block reaches.
All inputs are finite; a program needn't handle non-finite values.
Results may differ from the reference program's by a relative error of at most 0.0057.
Values may be sent and summed in bfloat16 or wider, within the bound.
No kernel may reach another device: no remote copies, remote signals or barrier semaphores. Data moves between devices by JAX's collectives and lax.ppermute only.
A program may use at most 192 MiB of HBM per device.

```python
import math
import jax
import jax.numpy as jnp
import numpy as np
from jax import lax

D = 6144
FF = 6144
EXPERTS = 8
TOPK = 4
TOK_DEV = 8
TOKENS = 64
MOST = 5
CPD = 3072
QKVC = 4096


def draw_tokens(key, part):
    key = jax.random.fold_in(key, 17)
    base_key, row_key, col_key = jax.random.split(key, 3)
    row_scale = 10.0 ** jax.random.uniform(row_key, (TOKENS, 1), jnp.float32, -0.5, 0.5)
    ramp = jnp.arange(D, dtype=jnp.float32) / D - 0.5
    col_scale = 10.0 ** jax.random.uniform(col_key, (1, D), jnp.float32, -0.5, 0.5) * (3.0 ** ramp)[None, :]
    base = jnp.clip(jax.random.normal(base_key, (TOKENS, D), jnp.float32), -4.0, 4.0)
    return (base * row_scale * col_scale).astype(jnp.bfloat16)


def shard_levels(own_key, dims, cuts, smallest, high):
    def one(axis_at, shards_of):
        steps = jax.random.uniform(jax.random.fold_in(jax.random.fold_in(own_key, 6), axis_at), (shards_of,), jnp.float32, smallest / len(cuts), high / len(cuts))
        return jnp.repeat(jnp.exp(steps), dims[axis_at] // shards_of).reshape((-1,) + (1,) * (len(dims) - axis_at - 1))

    factor_of = one(*cuts[0])
    for cut in cuts[1:]:
        factor_of = factor_of * one(*cut)
    return factor_of


def shared_out(key, own, number, rows, number_of, top, limit, lean):
    order = jax.random.permutation(key, number_of)
    heavy_load, usual = load_shares(number_of, rows * top, limit, lean, True), load_shares(number_of, rows * top, limit, lean, False)
    places = jnp.arange(number_of)

    def named(tallies, turn):
        used = int((tallies > 0).sum())
        fixed = max(1, used // 4)
        passed = fixed + (places - fixed + turn * (used - fixed)) % max(1, number_of - fixed)
        return jnp.zeros((number_of,), jnp.int32).at[order[jnp.where(places < fixed, places, passed)]].set(jnp.asarray(tallies, jnp.int32))

    tallies = jnp.where(number % 4 == 0, named(heavy_load, number // 4), named(usual, number - number // 4 - 1))
    mixed = jax.random.permutation(jax.random.fold_in(own, 3), number_of)
    donor, taker = mixed[0:number_of // 2 * 2:2], mixed[1:number_of // 2 * 2:2]
    margin = jnp.minimum(tallies[donor] - 1, limit - tallies[taker]) // 2
    margin = jnp.where((donor == order[0]) | (taker == order[0]) | (tallies[taker] == 0), 0, jnp.maximum(margin, 0))
    passed = jax.random.randint(jax.random.fold_in(own, 4), (number_of // 2,), 0, 1 << 20) % (margin + 1)
    tallies = tallies.at[donor].add(-passed).at[taker].add(passed)
    labels = jnp.searchsorted(jnp.cumsum(tallies), jnp.arange(rows * top), side="right").astype(jnp.int32)
    grid = labels.reshape(top, rows).T
    grid = grid[jax.random.permutation(jax.random.fold_in(own, 1), rows)]
    turn = jax.random.randint(jax.random.fold_in(own, 2), (rows, 1), 0, top)
    return jnp.take_along_axis(grid, (jnp.arange(top)[None, :] + turn) % top, axis=1)


def load_shares(count, total, reach, skew, full):
    loads = [(1 << 20) // math.isqrt(rank ** skew) + 1 for rank in range(1, count + 1)]
    largest = reach if full else min(reach, max(-(-total // count), total * loads[0] // sum(loads)))
    least = 1 if total - largest >= count - 1 else 0
    holding, rest = [largest] + [least] * (count - 1), total - largest - least * (count - 1)
    while rest > 0:
        movable = [i for i in range(1, count) if holding[i] < largest] or [i for i in range(1, count) if holding[i] < reach]
        mass, left = sum([loads[i] for i in movable]), rest
        for i in movable:
            more = min(reach - holding[i], max(1, left * loads[i] // mass), rest)
            holding[i] = holding[i] + more
            rest = rest - more
    return np.array(holding)


def bell_draw(own_key, shape, scale, bound, cuts=(), held_as=jnp.bfloat16):
    gain = shard_levels(own_key, shape, cuts, -0.22, 0.18) if cuts else 1.0
    drawn = jax.random.normal(own_key, shape, jnp.float32) * scale * gain
    return jnp.minimum(jnp.maximum(drawn, -bound), bound).astype(held_as)


def setup_inputs(seed: int = 0, part: int = 0) -> dict:
    key_list = jax.random.split(jax.random.key(seed), 8)
    part_splits = jax.random.split(jax.random.fold_in(key_list[7], part), 8)
    tokens = draw_tokens(jax.random.fold_in(jax.random.fold_in(key_list[7], part), 71), part)
    norm_gain = jnp.clip(1.0 + 0.1 * jax.random.normal(key_list[1], (D,), jnp.float32), 0.5, 1.5)
    expert_ids_keys = jax.random.split(jax.random.fold_in(part_splits[2], 1), TOKENS // TOK_DEV)
    expert_ids_turns = jax.random.permutation(jax.random.fold_in(part_splits[2], 3), TOKENS // TOK_DEV)
    expert_ids = jax.vmap(lambda own, number: shared_out(jax.random.fold_in(part_splits[2], 2), own, number, TOK_DEV, EXPERTS, TOPK, MOST, 2))(expert_ids_keys, expert_ids_turns).reshape((TOKENS, TOPK))
    route_weight = jnp.clip(jnp.exp(math.log(1.0) - 2.9957323 * jax.random.uniform(part_splits[3], (TOKENS, TOPK), jnp.float32) ** shard_levels(part_splits[3], (TOKENS, TOPK), ((0, 8),), -0.2, 0.2)), 0.05, 1.0)
    w_up = bell_draw(key_list[4], (D, EXPERTS * FF), D ** -0.5, 0.078125, ((1, 16),))
    w_down = bell_draw(key_list[5], (EXPERTS * FF, D), (FF // 4) ** -0.5, 0.15625, ((0, 16),))
    w_qkv = bell_draw(key_list[6], (D, QKVC), D ** -0.5, 0.078125, ((0, 2), (1, 8)))
    return {"tokens": tokens, "norm_gain": norm_gain, "expert_ids": expert_ids, "route_weight": route_weight, "w_up": w_up, "w_down": w_down, "w_qkv": w_qkv}


def reference(tokens, norm_gain, expert_ids, route_weight, w_up, w_down, w_qkv):
    blocks = TOKENS // TOK_DEV
    assign = TOK_DEV * TOPK
    ids = expert_ids.reshape(blocks, assign)
    expert_hot = (ids[:, :, None] == jnp.arange(EXPERTS, dtype=jnp.int32)[None, None, :]).astype(jnp.int32)
    earlier = jnp.cumsum(expert_hot, axis=1) - expert_hot
    rank = lax.optimization_barrier(jnp.sum(earlier * expert_hot, axis=2))
    slot_key = ids * MOST + rank
    select = (slot_key[:, :, None] == jnp.arange(EXPERTS * MOST, dtype=jnp.int32)[None, None, :]).astype(jnp.float32)
    owner_row = jnp.arange(assign, dtype=jnp.int32) // TOPK
    row_hot = (owner_row[:, None] == jnp.arange(TOK_DEV, dtype=jnp.int32)[None, :]).astype(jnp.float32)
    placing = jnp.einsum('bas,ar->bsr', select, row_hot)
    rows = tokens.reshape(blocks, TOK_DEV, D).astype(jnp.float32)
    slots = jnp.einsum('bsr,brd->bsd', placing, rows).astype(jnp.bfloat16)
    slots = slots.reshape(blocks, EXPERTS, MOST, D)
    piece_width = min(FF, CPD)
    pieces = FF // piece_width

    def expert_out(expert):
        expert = expert.astype(jnp.int32)
        block_rows = lax.dynamic_index_in_dim(slots, expert, 1, keepdims=False).reshape(blocks * MOST, D)
        up_cols = lax.dynamic_slice_in_dim(w_up, expert * FF, FF, 1)
        up = jnp.dot(block_rows, up_cols, preferred_element_type=jnp.float32)
        hidden = jax.nn.silu(up).astype(jnp.bfloat16)
        down_rows = lax.dynamic_slice_in_dim(w_down, expert * FF, FF, 0)
        partial_value = jnp.einsum('rpc,pcd->rpd', hidden.reshape(blocks * MOST, pieces, piece_width).astype(jnp.float32), down_rows.reshape(pieces, piece_width, D).astype(jnp.float32))
        rounded = lax.optimization_barrier(partial_value.astype(jnp.bfloat16))
        return lax.optimization_barrier(jnp.sum(rounded.astype(jnp.float32), axis=1)).reshape(blocks, MOST, D)
    outputs = lax.map(expert_out, jnp.arange(EXPERTS, dtype=jnp.int32))
    outputs = jnp.transpose(outputs, (1, 0, 2, 3)).reshape(blocks, EXPERTS * MOST, D)
    shares = route_weight / lax.optimization_barrier(jnp.sum(route_weight, axis=1, keepdims=True))
    gates = lax.optimization_barrier(shares.astype(jnp.bfloat16)).astype(jnp.float32).reshape(blocks, assign)
    weighting = jnp.einsum('bas,ar->brs', select * gates[:, :, None], row_hot)
    moe = jnp.einsum('brs,bsd->brd', weighting, outputs).reshape(TOKENS, D)
    mixed = tokens.astype(jnp.float32) + moe
    squares = lax.optimization_barrier(jnp.sum(mixed * mixed, axis=1))
    scale = lax.rsqrt(squares / D + 1e-05)
    normed = (mixed * scale[:, None] * norm_gain[None, :]).astype(jnp.bfloat16)
    return jnp.dot(normed, w_qkv, preferred_element_type=jnp.float32).astype(jnp.bfloat16)
```

```python
import functools

import jax
import jax.numpy as jnp
from jax import lax
from jax.experimental import pallas as pl
from jax.experimental.pallas import tpu as pltpu
from jax.sharding import PartitionSpec as P

FF = 6144
EXPERTS = 8
EPSILON = 1e-05
LANES = 128
MIB = 1 << 20


def expert_index(col_count):
    place = lax.axis_index("ep") * lax.axis_size("tp") + lax.axis_index("tp")
    place = place * lax.axis_size("dp") + lax.axis_index("dp")
    return place * col_count // FF


def pack_kernel(tokens_ref, ids_ref, weight_ref, out_ref):
    rows, width = tokens_ref.shape
    out_ref[:, :width] = tokens_ref[...]
    weight = weight_ref[...]
    gates = (weight / jnp.sum(weight, axis=1, keepdims=True)).astype(jnp.bfloat16)
    gates = gates.astype(jnp.float32)
    ids = ids_ref[...]
    column = lax.broadcasted_iota(jnp.int32, (rows, LANES), 1)
    spread = jnp.zeros((rows, LANES), jnp.float32)
    for k in range(ids.shape[1]):
        spread += jnp.where(column == ids[:, k : k + 1], gates[:, k : k + 1], 0.0)
    out_ref[:, width:] = spread.astype(jnp.bfloat16)


def chunk_plan(width, pieces):
    n_tp, n_dp = pieces
    piece = width // (n_tp * n_dp)
    parts = max(1, -(-piece // 512))
    plan = [(jt, jd, part) for jd in reversed(range(n_dp)) for jt in reversed(range(n_tp)) for part in range(parts)]
    ring = min(4, len(plan))
    held = min(2, len(plan) - ring)
    return piece, piece // parts, plan, ring, held


def chunk_start(entry, piece, part_width, pieces):
    jt, jd, part = entry
    n_tp, n_dp = pieces
    at_tp = lax.rem(lax.axis_index("tp") + jt, n_tp)
    at_dp = lax.rem(lax.axis_index("dp") + jd, n_dp)
    return pl.multiple_of((at_tp * n_dp + at_dp) * piece + part * part_width, LANES)


def load_kernel(pieces, w_up_ref, w_down_ref, up_ref, held_ref, up_sem, held_sem):
    width = w_down_ref.shape[1]
    piece, part_width, plan, ring, held = chunk_plan(width, pieces)
    blocks = up_sem.shape[0]
    depth = w_up_ref.shape[0] // blocks
    copies = [
        pltpu.make_async_copy(
            w_up_ref.at[pl.ds(b * depth, depth), :], up_ref.at[pl.ds(b * depth, depth), :], up_sem.at[b]
        )
        for b in range(blocks)
    ]
    for h in range(held):
        start = chunk_start(plan[ring + h], piece, part_width, pieces)
        copies.append(
            pltpu.make_async_copy(w_down_ref.at[:, pl.ds(start, part_width)], held_ref.at[h], held_sem.at[h])
        )
    for copy in copies:
        copy.start()
    for copy in copies:
        copy.wait()


def expert_kernel(pieces, x_ref, up_ref, held_ref, w_down_ref, *refs):
    n_tp, n_dp = pieces
    outs, (hidden, slots, sem) = refs[:n_dp], refs[n_dp:]
    width = w_down_ref.shape[1]
    piece, part_width, plan, ring, held = chunk_plan(width, pieces)
    cols = up_ref.shape[1]
    rows = x_ref.shape[0]

    def fetch(at, slot):
        start = chunk_start(plan[at], piece, part_width, pieces)
        return pltpu.make_async_copy(w_down_ref.at[:, pl.ds(start, part_width)], slots.at[slot], sem.at[slot])

    for at in range(ring):
        fetch(at, at).start()

    step = 512 if cols % 512 == 0 else cols

    @pl.loop(0, cols // step)
    def _(i):
        at = pl.ds(pl.multiple_of(i * step, step), step)
        up = jnp.dot(x_ref[:, :width], up_ref[:, at], preferred_element_type=jnp.float32)
        hidden[:, at] = (up / (1.0 + jnp.exp(-up))).astype(jnp.bfloat16)

    mine = expert_index(cols)
    column = lax.broadcasted_iota(jnp.int32, (rows, LANES), 1)
    gate = jnp.sum(
        jnp.where(column == mine, x_ref[:, width:].astype(jnp.float32), 0.0), axis=1, keepdims=True
    )
    slot_of = {}
    free = []
    later = list(range(ring + held, len(plan)))
    for at in range(ring):
        slot_of[at] = at
    for at, (jt, jd, part) in enumerate(plan):
        if at in slot_of:
            slot = slot_of[at]
            fetch(at, slot).wait()
            block = slots[slot]
        else:
            block = held_ref[at - ring]
        value = jnp.dot(hidden[...], block, preferred_element_type=jnp.float32) * gate
        outs[jd][jt, :, part * part_width : (part + 1) * part_width] = value.astype(jnp.bfloat16)
        if at in slot_of and later:
            after = later.pop(0)
            slot_of[after] = slot_of[at]
            fetch(after, slot_of[at]).start()


def project_kernel(n_dp, *refs):
    xs, (inverse_ref, w_ref, out_ref, square_ref) = refs[:n_dp], refs[n_dp:]
    piece = xs[0].shape[1]
    total = None
    square = None
    for j, x_ref in enumerate(xs):
        at = lax.rem(lax.axis_index("dp") + n_dp - j, n_dp)
        rows = pl.ds(pl.multiple_of(at * piece, piece), piece)
        x = x_ref[...]
        term = jnp.dot(x, w_ref[rows, :], preferred_element_type=jnp.float32)
        plain = x.astype(jnp.float32) * inverse_ref[:, rows]
        part = jnp.sum(plain * plain, axis=1, keepdims=True)
        total = term if total is None else total + term
        square = part if square is None else square + part
    out_ref[...] = total
    square_ref[...] = jnp.broadcast_to(square, square_ref.shape)


def shift(x, axis, by):
    size = lax.axis_size(axis)
    return lax.ppermute(x, axis, [(i, (i + by) % size) for i in range(size)])


def flip(x, axis, bit):
    size = lax.axis_size(axis)
    return lax.ppermute(x, axis, [(i, i ^ bit) for i in range(size)])


VMEM = pl.BlockSpec(memory_space=pltpu.VMEM)
ANY = pl.BlockSpec(memory_space=pl.ANY)


def params(mib, **more):
    return pltpu.CompilerParams(vmem_limit_bytes=mib * MIB, **more)


def body(tokens, norm_gain, expert_ids, route_weight, w_up, w_down, w_qkv):
    n_ep, n_tp, n_dp = (lax.axis_size(a) for a in ("ep", "tp", "dp"))
    ep_index, tp_index, dp_index = (lax.axis_index(a) for a in ("ep", "tp", "dp"))
    rows_here, width = tokens.shape
    cols = w_up.shape[1]
    pieces = (n_tp, n_dp)
    piece, part_width, plan, ring, held = chunk_plan(width, pieces)
    rows = rows_here * n_ep * n_dp

    packed = pl.pallas_call(
        pack_kernel,
        out_shape=jax.ShapeDtypeStruct((rows_here, width + LANES), jnp.bfloat16),
        in_specs=[VMEM] * 3,
        out_specs=VMEM,
        compiler_params=params(1),
    )(tokens, expert_ids, route_weight)
    gathered = lax.all_gather(packed, ("ep", "dp"), axis=0, tiled=True)

    up_here, held_here = pl.pallas_call(
        functools.partial(load_kernel, pieces),
        out_shape=(
            pltpu.VMEM((width, cols), jnp.bfloat16),
            pltpu.VMEM((held, w_down.shape[0], part_width), jnp.bfloat16),
        ),
        in_specs=[ANY, ANY],
        out_specs=(VMEM, VMEM),
        scratch_shapes=[pltpu.SemaphoreType.DMA((8,)), pltpu.SemaphoreType.DMA((held,))],
        compiler_params=params(1),
        cost_estimate=pl.CostEstimate(flops=0, transcendentals=0, bytes_accessed=50 * MIB),
    )(w_up, w_down)
    up_here = pltpu.with_memory_space_constraint(up_here, pltpu.VMEM)
    held_here = pltpu.with_memory_space_constraint(held_here, pltpu.VMEM)

    outs = pl.pallas_call(
        functools.partial(expert_kernel, pieces),
        out_shape=tuple(pltpu.VMEM((n_tp, rows, piece), jnp.bfloat16) for _ in range(n_dp)),
        in_specs=[VMEM, VMEM, VMEM, ANY],
        out_specs=tuple(VMEM for _ in range(n_dp)),
        scratch_shapes=[
            pltpu.VMEM((rows, cols), jnp.bfloat16),
            pltpu.VMEM((ring, w_down.shape[0], part_width), jnp.bfloat16),
            pltpu.SemaphoreType.DMA((ring,)),
        ],
        compiler_params=params(20),
        cost_estimate=pl.CostEstimate(flops=4 * rows * cols * width, transcendentals=rows * cols, bytes_accessed=24 * MIB),
    )(gathered, up_here, held_here, w_down)

    total = outs[0].astype(jnp.float32)
    for j in range(1, n_dp):
        total = total + shift(outs[j], "dp", j).astype(jnp.float32)
    here = total[0]
    for j in range(1, n_tp):
        here = here + shift(total[j].astype(jnp.bfloat16), "tp", j).astype(jnp.float32)
    bit = 1
    while bit < n_ep:
        here = here + flip(here.astype(jnp.bfloat16), "ep", bit).astype(jnp.float32)
        bit *= 2
    start = (tp_index * n_dp + dp_index) * piece
    mixed = here + lax.dynamic_slice_in_dim(gathered, start, piece, 1).astype(jnp.float32)
    gain = lax.dynamic_slice_in_dim(norm_gain, dp_index * piece, piece, 0)
    scaled = (mixed * gain[None, :]).astype(jnp.bfloat16)
    features = [scaled] + [shift(scaled, "dp", j) for j in range(1, n_dp)]
    out_cols = w_qkv.shape[1]
    projected, squares = pl.pallas_call(
        functools.partial(project_kernel, n_dp),
        out_shape=(
            jax.ShapeDtypeStruct((rows, out_cols), jnp.float32),
            jax.ShapeDtypeStruct((rows, LANES), jnp.float32),
        ),
        in_specs=[VMEM] * (n_dp + 2),
        out_specs=(VMEM, VMEM),
        compiler_params=params(16),
    )(*features, (1.0 / norm_gain)[None, :], w_qkv)
    both = jnp.concatenate([projected, squares], axis=1)
    share = rows // n_tp
    total = lax.dynamic_slice_in_dim(both, tp_index * share, share, 0)
    for j in range(1, n_tp):
        at = lax.rem(tp_index + j, n_tp) * share
        total = total + shift(lax.dynamic_slice_in_dim(both, at, share, 0), "tp", j)
    scale = lax.rsqrt(total[:, out_cols : out_cols + 1] / width + EPSILON)
    return (total[:, :out_cols] * scale).astype(jnp.bfloat16)


def solution(mesh):
    return jax.shard_map(
        body,
        mesh=mesh,
        in_specs=(
            P(("group", "ep", "dp"), None),
            P("tp"),
            P(("group", "ep", "dp"), None),
            P(("group", "ep", "dp"), None),
            P(None, ("ep", "tp", "dp")),
            P(("ep", "tp", "dp"), None),
            P("tp", ("ep", "dp")),
        ),
        out_specs=P(("group", "tp"), ("ep", "dp")),
        check_vma=False,
    )
```

```python
import functools

import jax
import jax.numpy as jnp
from jax import lax
from jax.experimental import pallas as pl
from jax.experimental.pallas import tpu as pltpu
from jax.sharding import PartitionSpec as P

FF = 6144
EXPERTS = 8
EPSILON = 1e-05
LANES = 128
MIB = 1 << 20


def expert_index(col_count):
    place = lax.axis_index("ep") * lax.axis_size("tp") + lax.axis_index("tp")
    place = place * lax.axis_size("dp") + lax.axis_index("dp")
    return place * col_count // FF


def pack_kernel(tokens_ref, ids_ref, weight_ref, out_ref, sem):
    rows, width = tokens_ref.shape
    copy = pltpu.make_async_copy(tokens_ref, out_ref.at[:, pl.ds(0, width)], sem)
    copy.start()
    weight = weight_ref[...]
    gates = (weight / jnp.sum(weight, axis=0, keepdims=True)).astype(jnp.bfloat16)
    gates = gates.astype(jnp.float32)
    row = lax.broadcasted_iota(jnp.int32, (rows, rows), 0)
    same = row == lax.broadcasted_iota(jnp.int32, (rows, rows), 1)
    column = lax.broadcasted_iota(jnp.int32, (rows, LANES), 1)
    spread = jnp.zeros((rows, LANES), jnp.float32)
    for k in range(ids_ref.shape[0]):
        named = jnp.sum(jnp.where(same, ids_ref[k : k + 1, :], 0), axis=1, keepdims=True)
        gate = jnp.sum(jnp.where(same, gates[k : k + 1, :], 0.0), axis=1, keepdims=True)
        spread += jnp.where(column == named, gate, 0.0)
    out_ref[:, width:] = spread.astype(jnp.bfloat16)
    copy.wait()


def up_plan(cols):
    step = 512 if cols % 512 == 0 else cols
    count = cols // step
    return step, count, max(1, count - 2)


def down_plan(width, pieces):
    n_tp, n_dp = pieces
    piece = width // (n_tp * n_dp)
    parts = max(1, -(-piece // 512))
    plan = [(jt, jd, part) for jd in reversed(range(n_dp)) for jt in reversed(range(n_tp)) for part in range(parts)]
    return piece, piece // parts, plan, min(4, len(plan))


def own_place(pieces, jt=0, jd=0):
    n_tp, n_dp = pieces
    at_tp = lax.rem(lax.axis_index("tp") + jt, n_tp)
    at_dp = lax.rem(lax.axis_index("dp") + jd, n_dp)
    return at_tp * n_dp + at_dp


def load_kernel(w_up_ref, blocks_ref, done_ref, sem):
    count, _, step = blocks_ref.shape
    copies = [
        pltpu.make_async_copy(w_up_ref.at[:, pl.ds(b * step, step)], blocks_ref.at[b], sem.at[b])
        for b in range(count)
    ]
    for copy in copies:
        copy.start()
    for copy in copies:
        copy.wait()
    done_ref[...] = jnp.zeros_like(done_ref)


def expert_kernel(pieces, n_parts, *refs):
    n_tp, n_dp = pieces
    parts, refs = refs[:n_parts], refs[n_parts:]
    early_ref, w_up_ref, w_down_ref, w_qkv_ref = refs[:4]
    outs, refs = refs[4 : 4 + n_dp], refs[4 + n_dp :]
    own_ref, qkv_ref, wide, x_ref, hidden, late_ref, slots, late_sem, slot_sem, qkv_sem = refs
    width, cols = w_up_ref.shape
    rows = x_ref.shape[0]
    step, count, early = up_plan(cols)
    piece, part_width, plan, ring = down_plan(width, pieces)

    def fetch_up(b):
        return pltpu.make_async_copy(
            w_up_ref.at[:, pl.ds(b * step, step)], late_ref.at[b - early], late_sem.at[b - early]
        )

    def fetch_down(at):
        jt, jd, part = plan[at]
        start = pl.multiple_of(own_place(pieces, jt, jd) * piece + part * part_width, LANES)
        return pltpu.make_async_copy(
            w_down_ref.at[:, pl.ds(start, part_width)], slots.at[at % ring], slot_sem.at[at % ring]
        )

    fetch_qkv = pltpu.make_async_copy(w_qkv_ref, qkv_ref, qkv_sem)
    for b in range(early, count):
        fetch_up(b).start()
    for at in range(ring):
        fetch_down(at).start()

    if n_parts == 1:
        x_ref[...] = parts[0][...]
    else:
        each = parts[0].shape[0]
        per_dp = n_parts // n_dp
        for i, part in enumerate(parts):
            shift_dp, flip_ep = divmod(i, per_dp)
            from_ep = lax.axis_index("ep") ^ flip_ep
            from_dp = lax.rem(lax.axis_index("dp") + n_dp - shift_dp, n_dp)
            at = pl.multiple_of((from_ep * n_dp + from_dp) * each, each)
            wide[pl.ds(at, each), :] = part[...].astype(jnp.float32)
        x_ref[...] = wide[...].astype(jnp.bfloat16)
    own_ref[...] = x_ref[:, pl.ds(pl.multiple_of(own_place(pieces) * piece, LANES), piece)]

    for b in range(count):
        if b >= early:
            fetch_up(b).wait()
        block = early_ref[b] if b < early else late_ref[b - early]
        up = jnp.dot(x_ref[:, :width], block, preferred_element_type=jnp.float32)
        hidden[:, b * step : (b + 1) * step] = (up / (1.0 + jnp.exp(-up))).astype(jnp.bfloat16)

    mine = expert_index(cols)
    column = lax.broadcasted_iota(jnp.int32, (rows, LANES), 1)
    gate = jnp.sum(
        jnp.where(column == mine, x_ref[:, width:].astype(jnp.float32), 0.0), axis=1, keepdims=True
    )
    for at, (jt, jd, part) in enumerate(plan):
        fetch_down(at).wait()
        value = jnp.dot(hidden[...], slots[at % ring], preferred_element_type=jnp.float32) * gate
        outs[jd][jt, :, part * part_width : (part + 1) * part_width] = value.astype(jnp.bfloat16)
        if at + ring < len(plan):
            fetch_down(at + ring).start()
            if at + ring == len(plan) - 1:
                fetch_qkv.start()
    if ring == len(plan):
        fetch_qkv.start()
    fetch_qkv.wait()


def project_kernel(pieces, *refs):
    n_tp, n_dp = pieces
    xs, refs = refs[:n_dp], refs[n_dp:]
    inverse_ref, w_ref, keep_ref, square_ref = refs[:4]
    sends, total_ref = refs[4 : 4 + n_tp - 1], refs[-1]
    piece = xs[0].shape[1]
    cols = w_ref.shape[1]
    total = None
    square = None
    for j, x_ref in enumerate(xs):
        at = lax.rem(lax.axis_index("dp") + n_dp - j, n_dp)
        rows = pl.ds(pl.multiple_of(at * piece, piece), piece)
        x = x_ref[...]
        term = jnp.dot(x, w_ref[rows, :], preferred_element_type=jnp.float32)
        plain = x.astype(jnp.float32) * inverse_ref[:, rows]
        part = jnp.sum(plain * plain, axis=1, keepdims=True)
        total = term if total is None else total + term
        square = part if square is None else square + part
    high = square.astype(jnp.bfloat16).astype(jnp.float32)
    middle = (square - high).astype(jnp.bfloat16).astype(jnp.float32)
    low = square - high - middle
    lane = lax.broadcasted_iota(jnp.int32, (square.shape[0], LANES), 1)
    tail = jnp.where(lane == 0, high, jnp.where(lane == 1, middle, jnp.where(lane == 2, low, 0.0)))
    total_ref[:, :cols] = total
    total_ref[:, cols:] = tail
    share = keep_ref.shape[0]
    tp_index = lax.axis_index("tp")
    mine = pl.ds(pl.multiple_of(tp_index * share, share), share)
    keep_ref[...] = total_ref[mine, :cols]
    square_ref[...] = total_ref[mine, cols:]
    for j, send_ref in enumerate(sends):
        theirs = lax.rem(tp_index + j + 1, n_tp)
        send_ref[...] = total_ref[pl.ds(pl.multiple_of(theirs * share, share), share), :].astype(jnp.bfloat16)


def shift(x, axis, by):
    size = lax.axis_size(axis)
    return lax.ppermute(x, axis, [(i, (i + by) % size) for i in range(size)])


def flip(x, axis, bits):
    size = lax.axis_size(axis)
    return lax.ppermute(x, axis, [(i, i ^ bits) for i in range(size)])


VMEM = pl.BlockSpec(memory_space=pltpu.VMEM)
ANY = pl.BlockSpec(memory_space=pl.ANY)
SCOPED = 31


def params(mib):
    return pltpu.CompilerParams(vmem_limit_bytes=mib * MIB)


def body(tokens, norm_gain, expert_ids, route_weight, w_up, w_down, w_qkv):
    n_ep, n_tp, n_dp = (lax.axis_size(a) for a in ("ep", "tp", "dp"))
    dp_index = lax.axis_index("dp")
    rows_here, width = tokens.shape
    cols = w_up.shape[1]
    pieces = (n_tp, n_dp)
    rows = rows_here * n_ep * n_dp
    step, count, early = up_plan(cols)
    piece, part_width, plan, ring = down_plan(width, pieces)

    packed = pl.pallas_call(
        pack_kernel,
        out_shape=jax.ShapeDtypeStruct((rows_here, width + LANES), jnp.bfloat16),
        in_specs=[ANY, VMEM, VMEM],
        out_specs=VMEM,
        scratch_shapes=[pltpu.SemaphoreType.DMA],
        compiler_params=params(SCOPED),
    )(tokens, expert_ids.T, route_weight.T)
    blocks, done = pl.pallas_call(
        load_kernel,
        out_shape=(
            pltpu.VMEM((early, width, step), jnp.bfloat16),
            jax.ShapeDtypeStruct((8, LANES), jnp.float32),
        ),
        in_specs=[ANY],
        out_specs=(VMEM, VMEM),
        scratch_shapes=[pltpu.SemaphoreType.DMA((early,))],
        compiler_params=params(SCOPED),
        cost_estimate=pl.CostEstimate(flops=0, transcendentals=0, bytes_accessed=2 * early * width * step),
    )(w_up)
    blocks = pltpu.with_memory_space_constraint(blocks, pltpu.VMEM)

    if n_ep <= 4:
        parts = {0: packed}
        for bits in reversed(range(1, n_ep)):
            parts[bits] = flip(packed, "ep", bits)
        parts = [parts[bits] for bits in range(n_ep)]
        parts = [lax.optimization_barrier((part, done))[0] for part in parts]
        parts = parts + [shift(part, "dp", j) for j in range(1, n_dp) for part in parts]
    else:
        parts = [lax.all_gather(packed, ("ep", "dp"), axis=0, tiled=True)]

    late = max(1, count - early)
    results = pl.pallas_call(
        functools.partial(expert_kernel, pieces, len(parts)),
        out_shape=(
            *(pltpu.VMEM((n_tp, rows, piece), jnp.bfloat16) for _ in range(n_dp)),
            pltpu.VMEM((rows, piece), jnp.bfloat16),
            pltpu.VMEM(w_qkv.shape, jnp.bfloat16),
        ),
        in_specs=[VMEM] * (len(parts) + 1) + [ANY] * 3,
        out_specs=tuple(VMEM for _ in range(n_dp + 2)),
        scratch_shapes=[
            pltpu.VMEM((rows, width + LANES), jnp.float32),
            pltpu.VMEM((rows, width + LANES), jnp.bfloat16),
            pltpu.VMEM((rows, cols), jnp.bfloat16),
            pltpu.VMEM((late, width, step), jnp.bfloat16),
            pltpu.VMEM((ring, cols, part_width), jnp.bfloat16),
            pltpu.SemaphoreType.DMA((late,)),
            pltpu.SemaphoreType.DMA((ring,)),
            pltpu.SemaphoreType.DMA,
        ],
        compiler_params=params(SCOPED),
        cost_estimate=pl.CostEstimate(
            flops=4 * rows * cols * width, transcendentals=rows * cols, bytes_accessed=2 * cols * width
        ),
    )(*parts, blocks, w_up, w_down, w_qkv)
    outs, own, qkv_weights = results[:n_dp], results[n_dp], results[n_dp + 1]

    total = outs[0].astype(jnp.float32)
    for j in range(1, n_dp):
        total = total + shift(outs[j], "dp", j).astype(jnp.float32)
    here = total[0]
    for j in range(1, n_tp):
        here = here + shift(total[j].astype(jnp.bfloat16), "tp", j).astype(jnp.float32)
    bit = 1
    while bit < n_ep:
        here = here + flip(here.astype(jnp.bfloat16), "ep", bit).astype(jnp.float32)
        bit *= 2
    mixed = here + own.astype(jnp.float32)
    gain = lax.dynamic_slice_in_dim(norm_gain, dp_index * piece, piece, 0)
    scaled = (mixed * gain[None, :]).astype(jnp.bfloat16)
    features = [scaled] + [shift(scaled, "dp", j) for j in range(1, n_dp)]
    out_cols = w_qkv.shape[1]
    share = rows // n_tp
    projected = pl.pallas_call(
        functools.partial(project_kernel, pieces),
        out_shape=(
            jax.ShapeDtypeStruct((share, out_cols), jnp.float32),
            jax.ShapeDtypeStruct((share, LANES), jnp.float32),
            *(jax.ShapeDtypeStruct((share, out_cols + LANES), jnp.bfloat16) for _ in range(n_tp - 1)),
        ),
        in_specs=[VMEM] * (n_dp + 2),
        out_specs=tuple(VMEM for _ in range(n_tp + 1)),
        scratch_shapes=[pltpu.VMEM((rows, out_cols + LANES), jnp.float32)],
        compiler_params=params(16),
    )(*features, (1.0 / norm_gain)[None, :], pltpu.with_memory_space_constraint(qkv_weights, pltpu.VMEM))
    total, squares = projected[0], projected[1]
    for j in range(1, n_tp):
        received = shift(projected[1 + j], "tp", j).astype(jnp.float32)
        total = total + received[:, :out_cols]
        squares = squares + received[:, out_cols:]
    scale = lax.rsqrt(jnp.sum(squares[:, :3], axis=1, keepdims=True) / width + EPSILON)
    return (total * scale).astype(jnp.bfloat16)


def solution(mesh):
    return jax.shard_map(
        body,
        mesh=mesh,
        in_specs=(
            P(("group", "ep", "dp"), None),
            P("tp"),
            P(("group", "ep", "dp"), None),
            P(("group", "ep", "dp"), None),
            P(None, ("ep", "tp", "dp")),
            P(("ep", "tp", "dp"), None),
            P("tp", ("ep", "dp")),
        ),
        out_specs=P(("group", "tp"), ("ep", "dp")),
        check_vma=False,
    )
```

```python
import functools

import jax
import jax.numpy as jnp
from jax import lax
from jax.experimental import pallas as pl
from jax.experimental.pallas import tpu as pltpu
from jax.sharding import PartitionSpec as P

FF = 6144
EXPERTS = 8
EPSILON = 1e-05
LANES = 128
MIB = 1 << 20


def expert_index(col_count):
    place = lax.axis_index("ep") * lax.axis_size("tp") + lax.axis_index("tp")
    place = place * lax.axis_size("dp") + lax.axis_index("dp")
    return place * col_count // FF


def pack_kernel(tokens_ref, ids_ref, weight_ref, out_ref, ids, weight, sem):
    rows, width = tokens_ref.shape
    copies = [
        pltpu.make_async_copy(ids_ref, ids, sem.at[0]),
        pltpu.make_async_copy(weight_ref, weight, sem.at[1]),
        pltpu.make_async_copy(tokens_ref, out_ref.at[:, pl.ds(0, width)], sem.at[2]),
    ]
    for copy in copies:
        copy.start()
    copies[0].wait()
    copies[1].wait()
    gates = (weight[...] / jnp.sum(weight[...], axis=0, keepdims=True)).astype(jnp.bfloat16)
    gates = gates.astype(jnp.float32)
    row = lax.broadcasted_iota(jnp.int32, (rows, rows), 0)
    same = row == lax.broadcasted_iota(jnp.int32, (rows, rows), 1)
    column = lax.broadcasted_iota(jnp.int32, (rows, LANES), 1)
    spread = jnp.zeros((rows, LANES), jnp.float32)
    for k in range(ids.shape[0]):
        named = jnp.sum(jnp.where(same, ids[k : k + 1, :], 0), axis=1, keepdims=True)
        gate = jnp.sum(jnp.where(same, gates[k : k + 1, :], 0.0), axis=1, keepdims=True)
        spread += jnp.where(column == named, gate, 0.0)
    out_ref[:, width:] = spread.astype(jnp.bfloat16)
    copies[2].wait()


def up_plan(cols):
    step = 512 if cols % 512 == 0 else cols
    count = cols // step
    return step, count, max(1, count - 2)


def down_plan(width, cols, pieces):
    n_tp, n_dp = pieces
    piece = width // (n_tp * n_dp)
    parts = max(1, -(-piece // 512))
    plan = [(jt, jd, part) for jd in reversed(range(n_dp)) for jt in reversed(range(n_tp)) for part in range(parts)]
    step, _, early = up_plan(cols)
    fits = piece // parts == step and width % cols == 0
    slots = max(1, len(plan) - early * (width // cols), 5) if fits else len(plan)
    return piece, piece // parts, plan, min(slots, len(plan))


def own_place(pieces, jt=0, jd=0):
    n_tp, n_dp = pieces
    at_tp = lax.rem(lax.axis_index("tp") + jt, n_tp)
    at_dp = lax.rem(lax.axis_index("dp") + jd, n_dp)
    return at_tp * n_dp + at_dp


def load_kernel(w_up_ref, blocks_ref, done_ref, sem):
    count, _, step = blocks_ref.shape
    copies = [
        pltpu.make_async_copy(w_up_ref.at[:, pl.ds(b * step, step)], blocks_ref.at[b], sem.at[b])
        for b in range(count)
    ]
    for copy in copies:
        copy.start()
    for copy in copies:
        copy.wait()
    done_ref[...] = jnp.zeros_like(done_ref)


def expert_kernel(pieces, n_parts, *refs):
    n_tp, n_dp = pieces
    parts, refs = refs[:n_parts], refs[n_parts:]
    w_up_ref, w_down_ref, w_qkv_ref = refs[1:4]
    outs, refs = refs[4 : 4 + n_dp], refs[4 + n_dp :]
    own_ref, qkv_ref, early_ref, wide, x_ref, hidden, late_ref, slots = refs[:8]
    late_sem, slot_sem, qkv_sem = refs[8:]
    width, cols = w_up_ref.shape
    rows = x_ref.shape[0]
    step, count, early = up_plan(cols)
    piece, part_width, plan, own_slots = down_plan(width, cols, pieces)
    per_block = width // cols

    def fetch_up(b):
        return pltpu.make_async_copy(
            w_up_ref.at[:, pl.ds(b * step, step)], late_ref.at[b - early], late_sem.at[b - early]
        )

    def slot(at):
        if at < own_slots:
            return slots.at[at]
        block, part = divmod(at - own_slots, per_block)
        return early_ref.at[block, pl.ds(part * cols, cols), :]

    def fetch_down(at):
        jt, jd, part = plan[at]
        start = pl.multiple_of(own_place(pieces, jt, jd) * piece + part * part_width, LANES)
        return pltpu.make_async_copy(w_down_ref.at[:, pl.ds(start, part_width)], slot(at), slot_sem.at[at])

    fetch_qkv = pltpu.make_async_copy(w_qkv_ref, qkv_ref, qkv_sem)
    for b in range(early, count):
        fetch_up(b).start()
    for at in range(own_slots):
        fetch_down(at).start()

    each = parts[0].shape[0]
    per_dp = n_parts // n_dp
    if n_parts == 1:
        wide[...] = parts[0][...].astype(jnp.float32)
    for i, part in enumerate(parts if n_parts > 1 else ()):
        shift_dp, flip_ep = divmod(i, per_dp)
        from_ep = lax.axis_index("ep") ^ flip_ep
        from_dp = lax.rem(lax.axis_index("dp") + n_dp - shift_dp, n_dp)
        at = pl.multiple_of((from_ep * n_dp + from_dp) * each, each)
        wide[pl.ds(at, each), :] = part[...].astype(jnp.float32)
    x_ref[...] = wide[...].astype(jnp.bfloat16)
    share = own_ref.shape[0]
    own_ref[...] = wide[
        pl.ds(pl.multiple_of(lax.axis_index("ep") * share, share), share),
        pl.ds(pl.multiple_of(own_place(pieces) * piece, LANES), piece),
    ]

    following = own_slots
    for b in range(count):
        if b >= early:
            fetch_up(b).wait()
        block = early_ref[b] if b < early else late_ref[b - early]
        up = jnp.dot(x_ref[:, :width], block, preferred_element_type=jnp.float32)
        hidden[:, b * step : (b + 1) * step] = (up / (1.0 + jnp.exp(-up))).astype(jnp.bfloat16)
        while following < len(plan) and (following - own_slots) // per_block <= b:
            fetch_down(following).start()
            following += 1
    fetch_qkv.start()

    mine = expert_index(cols)
    column = lax.broadcasted_iota(jnp.int32, (rows, LANES), 1)
    gate = jnp.sum(
        jnp.where(column == mine, x_ref[:, width:].astype(jnp.float32), 0.0), axis=1, keepdims=True
    )
    for at, (jt, jd, part) in enumerate(plan):
        fetch_down(at).wait()
        value = jnp.dot(hidden[...], slot(at)[...], preferred_element_type=jnp.float32) * gate
        outs[jd][jt, :, part * part_width : (part + 1) * part_width] = value.astype(jnp.bfloat16)
    fetch_qkv.wait()


def split_kernel(pieces, *refs):
    n_tp, n_dp = pieces
    parts, (keep_ref, *sends) = refs[:n_dp], refs[n_dp:]
    share = keep_ref.shape[0]
    n_ep = parts[0].shape[1] // share
    targets = [(jt, e) for jt in reversed(range(n_tp)) for e in reversed(range(n_ep))]
    for jt, e in targets:
        at = pl.ds(pl.multiple_of((lax.axis_index("ep") ^ e) * share, share), share)
        total = parts[0][jt, at, :].astype(jnp.float32)
        for part in parts[1:]:
            total = total + part[jt, at, :].astype(jnp.float32)
        if (jt, e) == (0, 0):
            keep_ref[...] = total
        else:
            sends[targets.index((jt, e))][...] = total.astype(jnp.bfloat16)


def feature_kernel(keep_ref, own_ref, gain_ref, *refs):
    received, out_ref = refs[:-1], refs[-1]
    piece = out_ref.shape[1]
    total = keep_ref[...]
    for part in received:
        total = total + part[...].astype(jnp.float32)
    at = pl.ds(pl.multiple_of(lax.axis_index("dp") * piece, piece), piece)
    out_ref[...] = ((total + own_ref[...]) * gain_ref[:, at]).astype(jnp.bfloat16)


def project_kernel(pieces, n_blocks, *refs):
    n_tp, n_dp = pieces
    xs, refs = refs[: n_dp * n_blocks], refs[n_dp * n_blocks :]
    gain_ref, w_ref, keep_ref, square_ref = refs[:4]
    sends, (total_ref, x_ref) = refs[4 : 4 + n_tp - 1], refs[-2:]
    share, piece = xs[0].shape
    cols = w_ref.shape[1]
    total = None
    square = None
    for j in range(n_dp):
        for e in range(n_blocks):
            source = lax.axis_index("ep") ^ e if n_blocks > 1 else 0
            x_ref[j, pl.ds(pl.multiple_of(source * share, share), share), :] = xs[j * n_blocks + e][...]
        at = lax.rem(lax.axis_index("dp") + n_dp - j, n_dp)
        rows = pl.ds(pl.multiple_of(at * piece, piece), piece)
        x = x_ref[j]
        term = jnp.dot(x, w_ref[rows, :], preferred_element_type=jnp.float32)
        plain = x.astype(jnp.float32) / gain_ref[:, rows]
        part = jnp.sum(plain * plain, axis=1, keepdims=True)
        total = term if total is None else total + term
        square = part if square is None else square + part
    high = square.astype(jnp.bfloat16).astype(jnp.float32)
    middle = (square - high).astype(jnp.bfloat16).astype(jnp.float32)
    low = square - high - middle
    lane = lax.broadcasted_iota(jnp.int32, (square.shape[0], LANES), 1)
    tail = jnp.where(lane == 0, high, jnp.where(lane == 1, middle, jnp.where(lane == 2, low, 0.0)))
    total_ref[:, :cols] = total
    total_ref[:, cols:] = tail
    share = keep_ref.shape[0]
    tp_index = lax.axis_index("tp")
    mine = pl.ds(pl.multiple_of(tp_index * share, share), share)
    keep_ref[...] = total_ref[mine, :cols]
    square_ref[...] = total_ref[mine, cols:]
    for j, send_ref in enumerate(sends):
        theirs = lax.rem(tp_index + j + 1, n_tp)
        send_ref[...] = total_ref[pl.ds(pl.multiple_of(theirs * share, share), share), :].astype(jnp.bfloat16)


def shift(x, axis, by):
    size = lax.axis_size(axis)
    return lax.ppermute(x, axis, [(i, (i + by) % size) for i in range(size)])


def flip(x, axis, bits):
    size = lax.axis_size(axis)
    return lax.ppermute(x, axis, [(i, i ^ bits) for i in range(size)])


def send(x, bits, by):
    n_ep, n_tp = lax.axis_size("ep"), lax.axis_size("tp")
    pairs = [
        (e * n_tp + t, (e ^ bits) * n_tp + (t + by) % n_tp) for e in range(n_ep) for t in range(n_tp)
    ]
    return lax.ppermute(x, ("ep", "tp"), pairs)


VMEM = pl.BlockSpec(memory_space=pltpu.VMEM)
ANY = pl.BlockSpec(memory_space=pl.ANY)
SCOPED = 33


def params(mib):
    return pltpu.CompilerParams(vmem_limit_bytes=mib * MIB)


def body(tokens, norm_gain, expert_ids, route_weight, w_up, w_down, w_qkv):
    n_ep, n_tp, n_dp = (lax.axis_size(a) for a in ("ep", "tp", "dp"))
    rows_here, width = tokens.shape
    cols = w_up.shape[1]
    pieces = (n_tp, n_dp)
    rows = rows_here * n_ep * n_dp
    step, count, early = up_plan(cols)
    piece, part_width, plan, own_slots = down_plan(width, cols, pieces)

    packed = pl.pallas_call(
        pack_kernel,
        out_shape=jax.ShapeDtypeStruct((rows_here, width + LANES), jnp.bfloat16),
        in_specs=[ANY, ANY, ANY],
        out_specs=VMEM,
        scratch_shapes=[
            pltpu.VMEM(expert_ids.shape[::-1], jnp.int32),
            pltpu.VMEM(expert_ids.shape[::-1], jnp.float32),
            pltpu.SemaphoreType.DMA((3,)),
        ],
        compiler_params=params(SCOPED),
    )(tokens, expert_ids.T, route_weight.T)
    blocks, done = pl.pallas_call(
        load_kernel,
        out_shape=(
            pltpu.VMEM((early, width, step), jnp.bfloat16),
            jax.ShapeDtypeStruct((8, LANES), jnp.float32),
        ),
        in_specs=[ANY],
        out_specs=(VMEM, VMEM),
        scratch_shapes=[pltpu.SemaphoreType.DMA((early,))],
        compiler_params=params(SCOPED),
        cost_estimate=pl.CostEstimate(flops=0, transcendentals=0, bytes_accessed=2 * early * width * step),
    )(w_up)
    blocks = pltpu.with_memory_space_constraint(blocks, pltpu.VMEM)

    if n_ep <= 4:
        parts = {0: packed}
        for bits in reversed(range(1, n_ep)):
            parts[bits] = flip(packed, "ep", bits)
        parts = [parts[bits] for bits in range(n_ep)]
        parts = [lax.optimization_barrier((part, done))[0] for part in parts]
        parts = parts + [shift(part, "dp", j) for j in range(1, n_dp) for part in parts]
    else:
        parts = [lax.all_gather(packed, ("ep", "dp"), axis=0, tiled=True)]

    late = max(1, count - early)
    share = rows_here * n_dp
    results = pl.pallas_call(
        functools.partial(expert_kernel, pieces, len(parts)),
        out_shape=(
            *(pltpu.VMEM((n_tp, rows, piece), jnp.bfloat16) for _ in range(n_dp)),
            pltpu.VMEM((share, piece), jnp.float32),
            pltpu.VMEM(w_qkv.shape, jnp.bfloat16),
            pltpu.VMEM(blocks.shape, jnp.bfloat16),
        ),
        in_specs=[VMEM] * (len(parts) + 1) + [ANY] * 3,
        out_specs=tuple(VMEM for _ in range(n_dp + 3)),
        scratch_shapes=[
            pltpu.VMEM((rows, width + LANES), jnp.float32),
            pltpu.VMEM((rows, width + LANES), jnp.bfloat16),
            pltpu.VMEM((rows, cols), jnp.bfloat16),
            pltpu.VMEM((late, width, step), jnp.bfloat16),
            pltpu.VMEM((own_slots, cols, part_width), jnp.bfloat16),
            pltpu.SemaphoreType.DMA((late,)),
            pltpu.SemaphoreType.DMA((len(plan),)),
            pltpu.SemaphoreType.DMA,
        ],
        input_output_aliases={len(parts): n_dp + 2},
        compiler_params=params(SCOPED),
        cost_estimate=pl.CostEstimate(
            flops=4 * rows * cols * width, transcendentals=rows * cols, bytes_accessed=2 * cols * width
        ),
    )(*parts, blocks, w_up, w_down, w_qkv)
    outs, own, qkv_weights = results[:n_dp], results[n_dp], results[n_dp + 1]

    cores = [outs[0]] + [shift(outs[j], "dp", j) for j in range(1, n_dp)]
    if n_ep <= 4:
        targets = [(jt, e) for jt in reversed(range(n_tp)) for e in reversed(range(n_ep))][:-1]
        keep, *sends = pl.pallas_call(
            functools.partial(split_kernel, pieces),
            out_shape=(
                jax.ShapeDtypeStruct((share, piece), jnp.float32),
                *(jax.ShapeDtypeStruct((share, piece), jnp.bfloat16) for _ in targets),
            ),
            in_specs=[VMEM] * n_dp,
            out_specs=tuple(VMEM for _ in range(len(targets) + 1)),
            compiler_params=params(4),
        )(*cores)
        received = [send(x, e, jt) for x, (jt, e) in zip(sends, targets)]
    else:
        total = sum(core.astype(jnp.float32) for core in cores)
        here = total[0]
        for j in range(1, n_tp):
            here = here + shift(total[j].astype(jnp.bfloat16), "tp", j).astype(jnp.float32)
        keep = lax.psum_scatter(here, "ep", scatter_dimension=0, tiled=True)
        received = []
    gain = norm_gain[None, :]
    scaled = pl.pallas_call(
        feature_kernel,
        out_shape=jax.ShapeDtypeStruct((share, piece), jnp.bfloat16),
        in_specs=[VMEM] * (3 + len(received)),
        out_specs=VMEM,
        compiler_params=params(4),
    )(keep, own, gain, *received)
    if n_ep <= 4:
        features = {0: scaled}
        for bits in reversed(range(1, n_ep)):
            features[bits] = flip(scaled, "ep", bits)
        features = [features[bits] for bits in range(n_ep)]
    else:
        features = [lax.all_gather(scaled, "ep", axis=0, tiled=True)]
    n_blocks = len(features)
    features = features + [shift(x, "dp", j) for j in range(1, n_dp) for x in features]
    out_cols = w_qkv.shape[1]
    share = rows // n_tp
    projected = pl.pallas_call(
        functools.partial(project_kernel, pieces, n_blocks),
        out_shape=(
            jax.ShapeDtypeStruct((share, out_cols), jnp.float32),
            jax.ShapeDtypeStruct((share, LANES), jnp.float32),
            *(jax.ShapeDtypeStruct((share, out_cols + LANES), jnp.bfloat16) for _ in range(n_tp - 1)),
        ),
        in_specs=[VMEM] * (len(features) + 2),
        out_specs=tuple(VMEM for _ in range(n_tp + 1)),
        scratch_shapes=[
            pltpu.VMEM((rows, out_cols + LANES), jnp.float32),
            pltpu.VMEM((n_dp, rows, piece), jnp.bfloat16),
        ],
        compiler_params=params(16),
    )(*features, gain, pltpu.with_memory_space_constraint(qkv_weights, pltpu.VMEM))
    total, squares = projected[0], projected[1]
    for j in range(1, n_tp):
        received = shift(projected[1 + j], "tp", j).astype(jnp.float32)
        total = total + received[:, :out_cols]
        squares = squares + received[:, out_cols:]
    scale = lax.rsqrt(jnp.sum(squares[:, :3], axis=1, keepdims=True) / width + EPSILON)
    return (total * scale).astype(jnp.bfloat16)


def solution(mesh):
    return jax.shard_map(
        body,
        mesh=mesh,
        in_specs=(
            P(("group", "ep", "dp"), None),
            P("tp"),
            P(("group", "ep", "dp"), None),
            P(("group", "ep", "dp"), None),
            P(None, ("ep", "tp", "dp")),
            P(("ep", "tp", "dp"), None),
            P("tp", ("ep", "dp")),
        ),
        out_specs=P(("group", "tp"), ("ep", "dp")),
        check_vma=False,
    )
```

```python
import functools

import jax
import jax.numpy as jnp
from jax import lax
from jax.experimental import pallas as pl
from jax.experimental.pallas import tpu as pltpu
from jax.sharding import PartitionSpec as P

FF = 6144
EXPERTS = 8
EPSILON = 1e-05
LANES = 128
MIB = 1 << 20


def expert_index(col_count):
    place = lax.axis_index("ep") * lax.axis_size("tp") + lax.axis_index("tp")
    place = place * lax.axis_size("dp") + lax.axis_index("dp")
    return place * col_count // FF


def pack_kernel(tokens_ref, ids_ref, weight_ref, out_ref, ids, weight, sem):
    rows, width = tokens_ref.shape
    copies = [
        pltpu.make_async_copy(ids_ref, ids, sem.at[0]),
        pltpu.make_async_copy(weight_ref, weight, sem.at[1]),
        pltpu.make_async_copy(tokens_ref, out_ref.at[:, pl.ds(0, width)], sem.at[2]),
    ]
    for copy in copies:
        copy.start()
    copies[0].wait()
    copies[1].wait()
    gates = (weight[...] / jnp.sum(weight[...], axis=0, keepdims=True)).astype(jnp.bfloat16)
    gates = gates.astype(jnp.float32)
    row = lax.broadcasted_iota(jnp.int32, (rows, rows), 0)
    same = row == lax.broadcasted_iota(jnp.int32, (rows, rows), 1)
    column = lax.broadcasted_iota(jnp.int32, (rows, LANES), 1)
    spread = jnp.zeros((rows, LANES), jnp.float32)
    for k in range(ids.shape[0]):
        named = jnp.sum(jnp.where(same, ids[k : k + 1, :], 0), axis=1, keepdims=True)
        gate = jnp.sum(jnp.where(same, gates[k : k + 1, :], 0.0), axis=1, keepdims=True)
        spread += jnp.where(column == named, gate, 0.0)
    out_ref[:, width:] = spread.astype(jnp.bfloat16)
    copies[2].wait()


def up_plan(cols):
    step = 512 if cols % 512 == 0 else cols
    count = cols // step
    early = max(1, count - 2)
    first = max(1, early - 1)
    return step, [group for group in (range(0, first), range(first, early)) if len(group)], count - early


def down_plan(width, pieces):
    n_tp, n_dp = pieces
    piece = width // (n_tp * n_dp)
    parts = max(1, -(-piece // 512))
    return piece, parts, [(jt, jd) for jt in reversed(range(n_tp)) for jd in reversed(range(n_dp))]


def own_place(pieces, jt=0, jd=0):
    n_tp, n_dp = pieces
    at_tp = lax.rem(lax.axis_index("tp") + jt, n_tp)
    at_dp = lax.rem(lax.axis_index("dp") + jd, n_dp)
    return at_tp * n_dp + at_dp


def load_kernel(group, *refs):
    w_up_ref, (blocks_ref, done_ref, sem) = refs[0], refs[-3:]
    step = blocks_ref.shape[2]
    copies = [
        pltpu.make_async_copy(w_up_ref.at[:, pl.ds(b * step, step)], blocks_ref.at[b], sem.at[b - group[0]])
        for b in group
    ]
    for copy in copies:
        copy.start()
    for copy in copies:
        copy.wait()
    done_ref[...] = jnp.zeros_like(done_ref)


def stack_kernel(*refs):
    for i, part in enumerate(refs[:-1]):
        refs[-1][i] = part[...]


def gather_kernel(pieces, *refs):
    n_dp = pieces[1]
    parts, (x_ref, own_ref, wide) = refs[1:-3], refs[-3:]
    n_blocks, each, _ = parts[0].shape
    for j, part in enumerate(parts):
        from_dp = lax.rem(lax.axis_index("dp") + n_dp - j, n_dp)
        for e in range(n_blocks):
            if n_blocks == 1:
                at = 0
            else:
                at = pl.multiple_of(((lax.axis_index("ep") ^ e) * n_dp + from_dp) * each, each)
            wide[pl.ds(at, each), :] = part[e].astype(jnp.float32)
    x_ref[...] = wide[...].astype(jnp.bfloat16)
    share, piece = own_ref.shape
    own_ref[...] = wide[
        pl.ds(pl.multiple_of(lax.axis_index("ep") * share, share), share),
        pl.ds(pl.multiple_of(own_place(pieces) * piece, LANES), piece),
    ]


def down_copy(pieces, stage, part, w_down_ref, slots, sem):
    width = w_down_ref.shape[1]
    piece, parts, plan = down_plan(width, pieces)
    jt, jd = plan[stage]
    part_width = piece // parts
    start = pl.multiple_of(own_place(pieces, jt, jd) * piece + part * part_width, LANES)
    return pltpu.make_async_copy(w_down_ref.at[:, pl.ds(start, part_width)], slots.at[part], sem.at[part])


def up_kernel(pieces, blocks_ref, x_ref, *refs):
    w_up_ref, w_down_ref, hidden_ref, gate_ref, out_ref, next_ref, late, slots = refs[:8]
    late_sem, slot_sem, next_sem = refs[8:]
    width, cols = w_up_ref.shape
    rows = x_ref.shape[0]
    step, _, n_late = up_plan(cols)
    parts = slots.shape[0]
    early = blocks_ref.shape[0]

    def late_copy(b):
        start = pl.multiple_of((early + b) * step, step)
        return pltpu.make_async_copy(w_up_ref.at[:, pl.ds(start, step)], late.at[b], late_sem.at[b])

    @pl.loop(0, n_late)
    def _(b):
        late_copy(b).start()

    @pl.loop(0, parts)
    def _(part):
        down_copy(pieces, 0, part, w_down_ref, slots, slot_sem).start()

    @pl.loop(0, parts)
    def _(part):
        down_copy(pieces, 1, part, w_down_ref, next_ref, next_sem).start()

    def activate(b, block):
        up = jnp.dot(x_ref[:, :width], block, preferred_element_type=jnp.float32)
        at = pl.multiple_of(b * step, LANES if step % LANES == 0 else step)
        hidden_ref[:, pl.ds(at, step)] = (up / (1.0 + jnp.exp(-up))).astype(jnp.bfloat16)

    @pl.loop(0, early)
    def _(b):
        activate(b, blocks_ref[b])

    @pl.loop(0, n_late)
    def _(b):
        late_copy(b).wait()
        activate(early + b, late[b])

    mine = expert_index(cols)
    column = lax.broadcasted_iota(jnp.int32, (rows, LANES), 1)
    gate = jnp.sum(
        jnp.where(column == mine, x_ref[:, width:].astype(jnp.float32), 0.0), axis=1, keepdims=True
    )
    gate_ref[...] = jnp.broadcast_to(gate, gate_ref.shape)

    @pl.loop(0, parts)
    def _(part):
        down_copy(pieces, 0, part, w_down_ref, slots, slot_sem).wait()
        work_part(part, hidden_ref, gate_ref, slots, out_ref)

    @pl.loop(0, parts)
    def _(part):
        down_copy(pieces, 1, part, w_down_ref, next_ref, next_sem).wait()


def work_part(part, hidden_ref, gate_ref, slots, out_ref):
    part_width = slots.shape[2]
    value = jnp.dot(hidden_ref[...], slots[part], preferred_element_type=jnp.float32) * gate_ref[:, :1]
    at = pl.multiple_of(part * part_width, LANES)
    out_ref[:, pl.ds(at, part_width)] = value.astype(out_ref.dtype)


def down_kernel(pieces, stage, hidden_ref, gate_ref, slots, w_down_ref, out_ref, next_ref, sem):
    parts = slots.shape[0]

    @pl.loop(0, parts)
    def _(part):
        down_copy(pieces, stage + 1, part, w_down_ref, next_ref, sem).start()

    @pl.loop(0, parts)
    def _(part):
        work_part(part, hidden_ref, gate_ref, slots, out_ref)

    @pl.loop(0, parts)
    def _(part):
        down_copy(pieces, stage + 1, part, w_down_ref, next_ref, sem).wait()


def last_down_kernel(pieces, hidden_ref, gate_ref, first_ref, w_down_ref, *refs):
    n_dp = pieces[1]
    outs, (slots, sem) = refs[:n_dp], refs[n_dp:]
    parts = first_ref.shape[0]
    before = len(down_plan(w_down_ref.shape[1], pieces)[2]) - n_dp
    for j in range(1, n_dp):

        @pl.loop(0, parts)
        def _(part, j=j):
            down_copy(pieces, before + j, part, w_down_ref, slots.at[j - 1], sem.at[j - 1]).start()

    @pl.loop(0, parts)
    def _(part):
        work_part(part, hidden_ref, gate_ref, first_ref, outs[0])

    for j in range(1, n_dp):

        @pl.loop(0, parts)
        def _(part, j=j):
            down_copy(pieces, before + j, part, w_down_ref, slots.at[j - 1], sem.at[j - 1]).wait()
            work_part(part, hidden_ref, gate_ref, slots.at[j - 1], outs[j])


def add_kernel(*refs):
    total = refs[0][...].astype(jnp.float32)
    for part in refs[1:-1]:
        total = total + part[...].astype(jnp.float32)
    refs[-1][...] = total.astype(refs[-1].dtype)


def split_kernel(n_in, *refs):
    parts, (keep_ref, *sends) = refs[:n_in], refs[n_in:]
    share = keep_ref.shape[0]
    for e in reversed(range(len(sends) + 1)):
        at = pl.ds(pl.multiple_of((lax.axis_index("ep") ^ e) * share, share), share)
        total = parts[0][at, :].astype(jnp.float32)
        for part in parts[1:]:
            total = total + part[at, :].astype(jnp.float32)
        if e:
            sends[e - 1][...] = total.astype(jnp.bfloat16)
        else:
            keep_ref[...] = total


def feature_kernel(keep_ref, own_ref, gain_ref, *refs):
    received, out_ref = refs[:-1], refs[-1]
    piece = out_ref.shape[1]
    total = keep_ref[...]
    for part in received:
        total = total + part[...].astype(jnp.float32)
    at = pl.ds(pl.multiple_of(lax.axis_index("dp") * piece, piece), piece)
    out_ref[...] = ((total + own_ref[...]) * gain_ref[:, at]).astype(jnp.bfloat16)


def order_kernel(*refs):
    blocks, out_ref = refs[:-1], refs[-1]
    share = blocks[0].shape[0]
    for e, block in enumerate(blocks):
        at = pl.multiple_of((lax.axis_index("ep") ^ e) * share, share)
        out_ref[pl.ds(at, share), :] = block[...]


def project_piece(n_dp, j, x_ref, gain_ref, w_ref):
    piece = x_ref.shape[1]
    at = lax.rem(lax.axis_index("dp") + n_dp - j, n_dp)
    rows = pl.ds(pl.multiple_of(at * piece, piece), piece)
    x = x_ref[...]
    plain = x.astype(jnp.float32) / gain_ref[:, rows]
    product = jnp.dot(x, w_ref[rows, :], preferred_element_type=jnp.float32)
    return product, jnp.sum(plain * plain, axis=1, keepdims=True)


def first_project_kernel(n_dp, x_ref, gain_ref, w_ref, out_ref):
    cols = w_ref.shape[1]
    product, square = project_piece(n_dp, 0, x_ref, gain_ref, w_ref)
    out_ref[:, :cols] = product
    out_ref[:, cols:] = jnp.broadcast_to(square, (square.shape[0], LANES))


def project_kernel(pieces, *refs):
    n_tp, n_dp = pieces
    others, refs = refs[: n_dp - 1], refs[n_dp - 1 :]
    first_ref, gain_ref, w_ref, keep_ref, square_ref = refs[:5]
    sends, total_ref = refs[5:-1], refs[-1]
    cols = w_ref.shape[1]
    total = first_ref[:, :cols]
    square = first_ref[:, cols : cols + 1]
    for j, x_ref in enumerate(others):
        term, part = project_piece(n_dp, j + 1, x_ref, gain_ref, w_ref)
        total = total + term
        square = square + part
    high = square.astype(jnp.bfloat16).astype(jnp.float32)
    middle = (square - high).astype(jnp.bfloat16).astype(jnp.float32)
    low = square - high - middle
    lane = lax.broadcasted_iota(jnp.int32, (square.shape[0], LANES), 1)
    tail = jnp.where(lane == 0, high, jnp.where(lane == 1, middle, jnp.where(lane == 2, low, 0.0)))
    total_ref[:, :cols] = total
    total_ref[:, cols:] = tail
    share = keep_ref.shape[0]
    tp_index = lax.axis_index("tp")
    mine = pl.ds(pl.multiple_of(tp_index * share, share), share)
    keep_ref[...] = total_ref[mine, :cols]
    square_ref[...] = total_ref[mine, cols:]
    for j, send_ref in enumerate(sends):
        theirs = lax.rem(tp_index + j + 1, n_tp)
        send_ref[...] = total_ref[pl.ds(pl.multiple_of(theirs * share, share), share), :].astype(jnp.bfloat16)


def shift(x, axis, by):
    size = lax.axis_size(axis)
    return lax.ppermute(x, axis, [(i, (i + by) % size) for i in range(size)])


def flip(x, axis, bits):
    size = lax.axis_size(axis)
    return lax.ppermute(x, axis, [(i, i ^ bits) for i in range(size)])


VMEM = pl.BlockSpec(memory_space=pltpu.VMEM)
ANY = pl.BlockSpec(memory_space=pl.ANY)
SCOPED = 24
SHARE = 1000


def params(mib):
    return pltpu.CompilerParams(vmem_limit_bytes=mib * MIB)


def cost(flops, bytes_accessed):
    return pl.CostEstimate(flops=flops // SHARE, transcendentals=0, bytes_accessed=bytes_accessed // SHARE)


def in_vmem(x):
    return pltpu.with_memory_space_constraint(x, pltpu.VMEM)


def body(tokens, norm_gain, expert_ids, route_weight, w_up, w_down, w_qkv):
    n_ep, n_tp, n_dp = (lax.axis_size(a) for a in ("ep", "tp", "dp"))
    rows_here, width = tokens.shape
    cols = w_up.shape[1]
    pieces = (n_tp, n_dp)
    rows = rows_here * n_ep * n_dp
    share = rows_here * n_dp
    step, groups, n_late = up_plan(cols)
    piece, n_parts, plan = down_plan(width, pieces)
    part_width = piece // n_parts
    direct = n_ep <= 4

    packed = pl.pallas_call(
        pack_kernel,
        out_shape=jax.ShapeDtypeStruct((rows_here, width + LANES), jnp.bfloat16),
        in_specs=[ANY, ANY, ANY],
        out_specs=VMEM,
        scratch_shapes=[
            pltpu.VMEM(expert_ids.shape[::-1], jnp.int32),
            pltpu.VMEM(expert_ids.shape[::-1], jnp.float32),
            pltpu.SemaphoreType.DMA((3,)),
        ],
        compiler_params=params(2),
    )(*(pltpu.with_memory_space_constraint(x, pltpu.HBM) for x in (tokens, expert_ids.T, route_weight.T)))

    def following(x, after):
        return lax.optimization_barrier((x, after))[0]

    early = sum(len(group) for group in groups)

    def load(group, after, *blocks):
        weights = following(w_up, after)
        return pl.pallas_call(
            functools.partial(load_kernel, group),
            out_shape=(
                pltpu.VMEM((early, width, step), jnp.bfloat16),
                jax.ShapeDtypeStruct((8, LANES), jnp.float32),
            ),
            in_specs=[ANY] + [VMEM] * len(blocks),
            out_specs=(VMEM, VMEM),
            scratch_shapes=[pltpu.SemaphoreType.DMA((len(group),))],
            input_output_aliases={1: 0} if blocks else {},
            compiler_params=params(SCOPED),
            cost_estimate=cost(0, 2 * len(group) * width * step),
        )(weights, *(in_vmem(block) for block in blocks))

    blocks, done = load(groups[0], packed)
    if direct:
        parts = [packed] + [None] * (n_ep - 1)
        for bits in reversed(range(1, n_ep)):
            parts[bits] = flip(packed, "ep", bits)
        parts = [following(part, done) for part in parts]
        stacked = pl.pallas_call(
            stack_kernel,
            out_shape=jax.ShapeDtypeStruct((n_ep, rows_here, width + LANES), jnp.bfloat16),
            in_specs=[VMEM] * n_ep,
            out_specs=VMEM,
            compiler_params=params(4),
        )(*parts)
        if len(groups) > 1:
            blocks, done = load(groups[1], stacked, blocks)
        parts = [stacked] + [following(shift(stacked, "dp", j), done) for j in range(1, n_dp)]
    else:
        for group in groups[1:]:
            blocks, done = load(group, done, blocks)
        parts = [lax.all_gather(packed, ("ep", "dp"), axis=0, tiled=True)[None]]

    x, own = pl.pallas_call(
        functools.partial(gather_kernel, pieces),
        out_shape=(
            pltpu.VMEM((rows, width + LANES), jnp.bfloat16),
            jax.ShapeDtypeStruct((share, piece), jnp.float32),
        ),
        in_specs=[VMEM] * (len(parts) + 1),
        out_specs=(VMEM, VMEM),
        scratch_shapes=[pltpu.VMEM((rows, width + LANES), jnp.float32)],
        compiler_params=params(SCOPED),
    )(in_vmem(blocks), *parts)

    units = pltpu.VMEM((n_parts, cols, part_width), jnp.bfloat16)
    hidden, gate, out, slots = pl.pallas_call(
        functools.partial(up_kernel, pieces),
        out_shape=(
            pltpu.VMEM((rows, cols), jnp.bfloat16),
            pltpu.VMEM((rows, LANES), jnp.float32),
            pltpu.VMEM((rows, piece), jnp.bfloat16),
            units,
        ),
        in_specs=[VMEM] * 2 + [ANY] * 2,
        out_specs=(VMEM,) * 4,
        scratch_shapes=[
            pltpu.VMEM((max(1, n_late), width, step), jnp.bfloat16),
            units,
            pltpu.SemaphoreType.DMA((max(1, n_late),)),
            pltpu.SemaphoreType.DMA((n_parts,)),
            pltpu.SemaphoreType.DMA((n_parts,)),
        ],
        compiler_params=params(SCOPED),
        cost_estimate=cost(2 * rows * cols * (width + piece), 24 * MIB),
    )(in_vmem(blocks), in_vmem(x), w_up, w_down)

    received = []
    gathering = [shift(out, "dp", plan[0][1])] if plan[0][1] else []
    after = out
    shared = dict(compiler_params=params(12), cost_estimate=cost(2 * rows * cols * piece, 2 * cols * piece))
    for stage in range(1, len(plan) - n_dp):
        jt, jd = plan[stage]
        out, slots = pl.pallas_call(
            functools.partial(down_kernel, pieces, stage),
            out_shape=(pltpu.VMEM((rows, piece), jnp.bfloat16 if jd else jnp.float32), units),
            in_specs=[VMEM] * 3 + [ANY],
            out_specs=(VMEM,) * 2,
            scratch_shapes=[pltpu.SemaphoreType.DMA((n_parts,))],
            **shared,
        )(in_vmem(hidden), in_vmem(gate), in_vmem(slots), following(w_down, after))
        if jd:
            gathering.append(shift(out, "dp", jd))
        else:
            after = pl.pallas_call(
                add_kernel,
                out_shape=jax.ShapeDtypeStruct((rows, piece), jnp.bfloat16),
                in_specs=[VMEM] * (1 + len(gathering)),
                out_specs=VMEM,
                compiler_params=params(4),
            )(out, *gathering)
            received.append(shift(after, "tp", jt))
            gathering = []
    *outs, out = pl.pallas_call(
        functools.partial(last_down_kernel, pieces),
        out_shape=tuple(
            pltpu.VMEM((rows, piece), jnp.bfloat16 if jd else jnp.float32) for jd in reversed(range(n_dp))
        ),
        in_specs=[VMEM] * 3 + [ANY],
        out_specs=(VMEM,) * n_dp,
        scratch_shapes=[
            pltpu.VMEM((max(1, n_dp - 1), n_parts, cols, part_width), jnp.bfloat16),
            pltpu.SemaphoreType.DMA((max(1, n_dp - 1), n_parts)),
        ],
        **shared,
    )(in_vmem(hidden), in_vmem(gate), in_vmem(slots), following(w_down, after))
    gathering = [shift(x, "dp", plan[len(plan) - n_dp + j][1]) for j, x in enumerate(outs)]
    kept = pl.pallas_call(
        add_kernel,
        out_shape=jax.ShapeDtypeStruct((rows, piece), jnp.float32),
        in_specs=[VMEM] * (1 + len(received)),
        out_specs=VMEM,
        compiler_params=params(4),
    )(out, *received)
    arrived = [kept, *gathering]
    if direct:
        keep, *sends = pl.pallas_call(
            functools.partial(split_kernel, len(arrived)),
            out_shape=(
                jax.ShapeDtypeStruct((share, piece), jnp.float32),
                *(jax.ShapeDtypeStruct((share, piece), jnp.bfloat16) for _ in range(n_ep - 1)),
            ),
            in_specs=[VMEM] * len(arrived),
            out_specs=(VMEM,) * n_ep,
            compiler_params=params(4),
        )(*arrived)
        received = [flip(sends[bits - 1], "ep", bits) for bits in reversed(range(1, n_ep))]
    else:
        total = sum(x.astype(jnp.float32) for x in arrived)
        keep = lax.psum_scatter(total, "ep", scatter_dimension=0, tiled=True)
        received = []
    gain = norm_gain[None, :]
    scaled = pl.pallas_call(
        feature_kernel,
        out_shape=jax.ShapeDtypeStruct((share, piece), jnp.bfloat16),
        in_specs=[VMEM] * (3 + len(received)),
        out_specs=VMEM,
        compiler_params=params(4),
    )(keep, own, gain, *received)
    if direct:
        blocks = [scaled] + [None] * (n_ep - 1)
        for bits in reversed(range(1, n_ep)):
            blocks[bits] = flip(scaled, "ep", bits)
        mine = pl.pallas_call(
            order_kernel,
            out_shape=jax.ShapeDtypeStruct((rows, piece), jnp.bfloat16),
            in_specs=[VMEM] * n_ep,
            out_specs=VMEM,
            compiler_params=params(4),
        )(*blocks)
    else:
        mine = lax.all_gather(scaled, "ep", axis=0, tiled=True)
    others = [shift(mine, "dp", j) for j in range(1, n_dp)]
    out_cols = w_qkv.shape[1]
    share = rows // n_tp
    first = pl.pallas_call(
        functools.partial(first_project_kernel, n_dp),
        out_shape=jax.ShapeDtypeStruct((rows, out_cols + LANES), jnp.float32),
        in_specs=[VMEM] * 3,
        out_specs=VMEM,
        compiler_params=params(12),
    )(mine, gain, w_qkv)
    projected = pl.pallas_call(
        functools.partial(project_kernel, pieces),
        out_shape=(
            jax.ShapeDtypeStruct((share, out_cols), jnp.float32),
            jax.ShapeDtypeStruct((share, LANES), jnp.float32),
            *(jax.ShapeDtypeStruct((share, out_cols + LANES), jnp.bfloat16) for _ in range(n_tp - 1)),
        ),
        in_specs=[VMEM] * (n_dp + 2),
        out_specs=tuple(VMEM for _ in range(n_tp + 1)),
        scratch_shapes=[pltpu.VMEM((rows, out_cols + LANES), jnp.float32)],
        compiler_params=params(12),
    )(*others, first, gain, w_qkv)
    total, squares = projected[0], projected[1]
    for j in range(1, n_tp):
        received = shift(projected[1 + j], "tp", j).astype(jnp.float32)
        total = total + received[:, :out_cols]
        squares = squares + received[:, out_cols:]
    scale = lax.rsqrt(jnp.sum(squares[:, :3], axis=1, keepdims=True) / width + EPSILON)
    return (total * scale).astype(jnp.bfloat16)


def solution(mesh):
    return jax.shard_map(
        body,
        mesh=mesh,
        in_specs=(
            P(("group", "ep", "dp"), None),
            P("tp"),
            P(("group", "ep", "dp"), None),
            P(("group", "ep", "dp"), None),
            P(None, ("ep", "tp", "dp")),
            P(("ep", "tp", "dp"), None),
            P("tp", ("ep", "dp")),
        ),
        out_specs=P(("group", "tp"), ("ep", "dp")),
        check_vma=False,
    )
```

```python
import functools

import jax
import jax.numpy as jnp
from jax import lax
from jax.experimental import pallas as pl
from jax.experimental.pallas import tpu as pltpu
from jax.sharding import PartitionSpec as P

FF = 6144
EXPERTS = 8
EPSILON = 1e-05
LANES = 128
MIB = 1 << 20


def expert_index(col_count):
    place = lax.axis_index("ep") * lax.axis_size("tp") + lax.axis_index("tp")
    place = place * lax.axis_size("dp") + lax.axis_index("dp")
    return place * col_count // FF


def pack_kernel(tokens_ref, ids_ref, weight_ref, out_ref, ids, weight, sem):
    rows, width = tokens_ref.shape
    copies = [
        pltpu.make_async_copy(ids_ref, ids, sem.at[0]),
        pltpu.make_async_copy(weight_ref, weight, sem.at[1]),
        pltpu.make_async_copy(tokens_ref, out_ref.at[:, pl.ds(0, width)], sem.at[2]),
    ]
    for copy in copies:
        copy.start()
    copies[0].wait()
    copies[1].wait()
    gates = (weight[...] / jnp.sum(weight[...], axis=0, keepdims=True)).astype(jnp.bfloat16)
    gates = gates.astype(jnp.float32)
    row = lax.broadcasted_iota(jnp.int32, (rows, rows), 0)
    same = row == lax.broadcasted_iota(jnp.int32, (rows, rows), 1)
    column = lax.broadcasted_iota(jnp.int32, (rows, LANES), 1)
    spread = jnp.zeros((rows, LANES), jnp.float32)
    for k in range(ids.shape[0]):
        named = jnp.sum(jnp.where(same, ids[k : k + 1, :], 0), axis=1, keepdims=True)
        gate = jnp.sum(jnp.where(same, gates[k : k + 1, :], 0.0), axis=1, keepdims=True)
        spread += jnp.where(column == named, gate, 0.0)
    out_ref[:, width:] = spread.astype(jnp.bfloat16)
    copies[2].wait()


def up_plan(cols):
    step = 1024 if cols % 1024 == 0 else cols
    count = cols // step
    early = max(1, count - 1)
    return step, [range(0, early)], count - early


def down_plan(width, pieces):
    n_tp, n_dp = pieces
    piece = width // (n_tp * n_dp)
    parts = max(1, -(-piece // 512))
    return piece, parts, [(jt, jd) for jt in reversed(range(n_tp)) for jd in reversed(range(n_dp))]


def own_place(pieces, jt=0, jd=0):
    n_tp, n_dp = pieces
    at_tp = lax.rem(lax.axis_index("tp") + jt, n_tp)
    at_dp = lax.rem(lax.axis_index("dp") + jd, n_dp)
    return at_tp * n_dp + at_dp


def load_kernel(group, *refs):
    w_up_ref, (blocks_ref, done_ref, sem) = refs[0], refs[-3:]
    step = blocks_ref.shape[2]
    copies = [
        pltpu.make_async_copy(w_up_ref.at[:, pl.ds(b * step, step)], blocks_ref.at[b], sem.at[b - group[0]])
        for b in group
    ]
    for copy in copies:
        copy.start()
    for copy in copies:
        copy.wait()
    done_ref[...] = jnp.zeros_like(done_ref)


def stack_kernel(*refs):
    for i, part in enumerate(refs[:-1]):
        refs[-1][i] = part[...]


def gather_kernel(pieces, *refs):
    n_dp = pieces[1]
    parts, (x_ref, own_ref, wide) = refs[1:-3], refs[-3:]
    n_blocks, each, _ = parts[0].shape
    for j, part in enumerate(parts):
        from_dp = lax.rem(lax.axis_index("dp") + n_dp - j, n_dp)
        for e in range(n_blocks):
            if n_blocks == 1:
                at = 0
            else:
                at = pl.multiple_of(((lax.axis_index("ep") ^ e) * n_dp + from_dp) * each, each)
            wide[pl.ds(at, each), :] = part[e].astype(jnp.float32)
    x_ref[...] = wide[...].astype(jnp.bfloat16)
    share, piece = own_ref.shape
    own_ref[...] = wide[
        pl.ds(pl.multiple_of(lax.axis_index("ep") * share, share), share),
        pl.ds(pl.multiple_of(own_place(pieces) * piece, LANES), piece),
    ]


def down_copy(pieces, stage, part, w_down_ref, slot, sem):
    piece, parts, plan = down_plan(w_down_ref.shape[1], pieces)
    jt, jd = plan[stage]
    part_width = piece // parts
    start = pl.multiple_of(own_place(pieces, jt, jd) * piece + part * part_width, LANES)
    return pltpu.make_async_copy(w_down_ref.at[:, pl.ds(start, part_width)], slot, sem)


def up_kernel(pieces, blocks_ref, x_ref, *refs):
    w_up_ref, w_down_ref, hidden_ref, gate_ref, out_ref, next_ref, late, slots = refs[:8]
    late_sem, slot_sem, next_sem = refs[8:]
    width, cols = w_up_ref.shape
    rows = x_ref.shape[0]
    step, _, n_late = up_plan(cols)
    parts = slots.shape[0]
    early = blocks_ref.shape[0]

    def late_copy(b):
        start = pl.multiple_of((early + b) * step, step)
        return pltpu.make_async_copy(w_up_ref.at[:, pl.ds(start, step)], late.at[b], late_sem.at[b])

    @pl.loop(0, n_late)
    def _(b):
        late_copy(b).start()

    @pl.loop(0, parts)
    def _(part):
        down_copy(pieces, 0, part, w_down_ref, slots.at[part], slot_sem.at[part]).start()

    @pl.loop(0, parts)
    def _(part):
        down_copy(pieces, 1, part, w_down_ref, next_ref.at[part], next_sem.at[part]).start()

    def activate(b, block):
        up = jnp.dot(x_ref[:, :width], block, preferred_element_type=jnp.float32)
        at = pl.multiple_of(b * step, LANES if step % LANES == 0 else step)
        hidden_ref[:, pl.ds(at, step)] = (up / (1.0 + jnp.exp(-up))).astype(jnp.bfloat16)

    @pl.loop(0, early)
    def _(b):
        activate(b, blocks_ref[b])

    @pl.loop(0, n_late)
    def _(b):
        late_copy(b).wait()
        activate(early + b, late[b])

    mine = expert_index(cols)
    column = lax.broadcasted_iota(jnp.int32, (rows, LANES), 1)
    gate = jnp.sum(
        jnp.where(column == mine, x_ref[:, width:].astype(jnp.float32), 0.0), axis=1, keepdims=True
    )
    gate_ref[...] = jnp.broadcast_to(gate, gate_ref.shape)

    @pl.loop(0, parts)
    def _(part):
        down_copy(pieces, 0, part, w_down_ref, slots.at[part], slot_sem.at[part]).wait()
        work_part(part, hidden_ref, gate_ref, slots[part], out_ref)

    @pl.loop(0, parts)
    def _(part):
        down_copy(pieces, 1, part, w_down_ref, next_ref.at[part], next_sem.at[part]).wait()


def work_part(part, hidden_ref, gate_ref, block, out_ref):
    part_width = block.shape[1]
    value = jnp.dot(hidden_ref[...], block, preferred_element_type=jnp.float32) * gate_ref[:, :1]
    at = pl.multiple_of(part * part_width, LANES)
    out_ref[:, pl.ds(at, part_width)] = value.astype(out_ref.dtype)


def down_kernel(pieces, stage, hidden_ref, gate_ref, slots, w_down_ref, out_ref, next_ref, sem):
    @pl.loop(0, next_ref.shape[0])
    def _(part):
        down_copy(pieces, stage + 1, part, w_down_ref, next_ref.at[part], sem.at[part]).start()

    @pl.loop(0, slots.shape[0])
    def _(part):
        work_part(part, hidden_ref, gate_ref, slots[part], out_ref)

    @pl.loop(0, next_ref.shape[0])
    def _(part):
        down_copy(pieces, stage + 1, part, w_down_ref, next_ref.at[part], sem.at[part]).wait()


def last_down_kernel(pieces, hidden_ref, gate_ref, first_ref, w_down_ref, *refs):
    n_dp = pieces[1]
    outs, (slots, sem) = refs[:n_dp], refs[n_dp:]
    held = first_ref.shape[0]
    _, parts, plan = down_plan(w_down_ref.shape[1], pieces)
    before = len(plan) - n_dp

    def copy(j, part):
        at = j * parts + part - held
        return down_copy(pieces, before + j, part, w_down_ref, slots.at[at], sem.at[at])

    for j in range(n_dp):

        @pl.loop(held if j == 0 else 0, parts)
        def _(part, j=j):
            copy(j, part).start()

    @pl.loop(0, held)
    def _(part):
        work_part(part, hidden_ref, gate_ref, first_ref[part], outs[0])

    for j in range(n_dp):

        @pl.loop(held if j == 0 else 0, parts)
        def _(part, j=j):
            copy(j, part).wait()
            work_part(part, hidden_ref, gate_ref, slots[j * parts + part - held], outs[j])


def add_kernel(*refs):
    total = refs[0][...].astype(jnp.float32)
    for part in refs[1:-1]:
        total = total + part[...].astype(jnp.float32)
    refs[-1][...] = total.astype(refs[-1].dtype)


def split_kernel(n_in, *refs):
    parts, (keep_ref, *sends) = refs[:n_in], refs[n_in:]
    share = keep_ref.shape[0]
    for e in reversed(range(len(sends) + 1)):
        at = pl.ds(pl.multiple_of((lax.axis_index("ep") ^ e) * share, share), share)
        total = parts[0][at, :].astype(jnp.float32)
        for part in parts[1:]:
            total = total + part[at, :].astype(jnp.float32)
        if e:
            sends[e - 1][...] = total.astype(jnp.bfloat16)
        else:
            keep_ref[...] = total


def feature_kernel(keep_ref, own_ref, gain_ref, *refs):
    received, out_ref = refs[:-1], refs[-1]
    piece = out_ref.shape[1]
    total = keep_ref[...]
    for part in received:
        total = total + part[...].astype(jnp.float32)
    at = pl.ds(pl.multiple_of(lax.axis_index("dp") * piece, piece), piece)
    out_ref[...] = ((total + own_ref[...]) * gain_ref[:, at]).astype(jnp.bfloat16)


def order_kernel(*refs):
    blocks, out_ref = refs[:-1], refs[-1]
    share = blocks[0].shape[0]
    for e, block in enumerate(blocks):
        at = pl.multiple_of((lax.axis_index("ep") ^ e) * share, share)
        out_ref[pl.ds(at, share), :] = block[...]


def project_piece(n_dp, j, x_ref, gain_ref, w_ref):
    piece = x_ref.shape[1]
    at = lax.rem(lax.axis_index("dp") + n_dp - j, n_dp)
    rows = pl.ds(pl.multiple_of(at * piece, piece), piece)
    x = x_ref[...]
    plain = x.astype(jnp.float32) * (1.0 / gain_ref[:, rows])
    product = jnp.dot(x, w_ref[rows, :], preferred_element_type=jnp.float32)
    return product, jnp.sum(plain * plain, axis=1, keepdims=True)


def first_project_kernel(n_dp, x_ref, gain_ref, w_ref, out_ref):
    cols = w_ref.shape[1]
    product, square = project_piece(n_dp, 0, x_ref, gain_ref, w_ref)
    out_ref[:, :cols] = product
    out_ref[:, cols:] = jnp.broadcast_to(square, (square.shape[0], LANES))


def project_kernel(pieces, *refs):
    n_tp, n_dp = pieces
    others, refs = refs[: n_dp - 1], refs[n_dp - 1 :]
    first_ref, gain_ref, w_ref, keep_ref, square_ref = refs[:5]
    sends, total_ref = refs[5:-1], refs[-1]
    cols = w_ref.shape[1]
    total = first_ref[:, :cols]
    square = first_ref[:, cols : cols + 1]
    for j, x_ref in enumerate(others):
        term, part = project_piece(n_dp, j + 1, x_ref, gain_ref, w_ref)
        total = total + term
        square = square + part
    high = square.astype(jnp.bfloat16).astype(jnp.float32)
    middle = (square - high).astype(jnp.bfloat16).astype(jnp.float32)
    low = square - high - middle
    lane = lax.broadcasted_iota(jnp.int32, (square.shape[0], LANES), 1)
    tail = jnp.where(lane == 0, high, jnp.where(lane == 1, middle, jnp.where(lane == 2, low, 0.0)))
    total_ref[:, :cols] = total
    total_ref[:, cols:] = tail
    share = keep_ref.shape[0]
    tp_index = lax.axis_index("tp")
    mine = pl.ds(pl.multiple_of(tp_index * share, share), share)
    keep_ref[...] = total_ref[mine, :cols]
    square_ref[...] = total_ref[mine, cols:]
    for j, send_ref in enumerate(sends):
        theirs = lax.rem(tp_index + j + 1, n_tp)
        send_ref[...] = total_ref[pl.ds(pl.multiple_of(theirs * share, share), share), :].astype(jnp.bfloat16)


def shift(x, axis, by):
    size = lax.axis_size(axis)
    return lax.ppermute(x, axis, [(i, (i + by) % size) for i in range(size)])


def flip(x, axis, bits):
    size = lax.axis_size(axis)
    return lax.ppermute(x, axis, [(i, i ^ bits) for i in range(size)])


def exchange_order(n_ep):
    return sorted(range(1, n_ep), key=lambda bits: (bits < n_ep // 2, bits))


VMEM = pl.BlockSpec(memory_space=pltpu.VMEM)
ANY = pl.BlockSpec(memory_space=pl.ANY)
SCOPED = 24
SHARE = 1000


def params(mib):
    return pltpu.CompilerParams(vmem_limit_bytes=mib * MIB)


def cost(flops, bytes_accessed):
    return pl.CostEstimate(flops=flops // SHARE, transcendentals=0, bytes_accessed=bytes_accessed // SHARE)


def in_vmem(x):
    return pltpu.with_memory_space_constraint(x, pltpu.VMEM)


def body(tokens, norm_gain, expert_ids, route_weight, w_up, w_down, w_qkv):
    n_ep, n_tp, n_dp = (lax.axis_size(a) for a in ("ep", "tp", "dp"))
    rows_here, width = tokens.shape
    cols = w_up.shape[1]
    pieces = (n_tp, n_dp)
    rows = rows_here * n_ep * n_dp
    share = rows_here * n_dp
    step, groups, n_late = up_plan(cols)
    piece, n_parts, plan = down_plan(width, pieces)
    part_width = piece // n_parts
    direct = n_ep <= 4

    packed = pl.pallas_call(
        pack_kernel,
        out_shape=jax.ShapeDtypeStruct((rows_here, width + LANES), jnp.bfloat16),
        in_specs=[ANY, ANY, ANY],
        out_specs=VMEM,
        scratch_shapes=[
            pltpu.VMEM(expert_ids.shape[::-1], jnp.int32),
            pltpu.VMEM(expert_ids.shape[::-1], jnp.float32),
            pltpu.SemaphoreType.DMA((3,)),
        ],
        compiler_params=params(2),
    )(*(pltpu.with_memory_space_constraint(x, pltpu.HBM) for x in (tokens, expert_ids.T, route_weight.T)))

    def following(x, after):
        return lax.optimization_barrier((x, after))[0]

    early = sum(len(group) for group in groups)

    def load(group, after, *blocks):
        weights = following(w_up, after)
        return pl.pallas_call(
            functools.partial(load_kernel, group),
            out_shape=(
                pltpu.VMEM((early, width, step), jnp.bfloat16),
                jax.ShapeDtypeStruct((8, LANES), jnp.float32),
            ),
            in_specs=[ANY] + [VMEM] * len(blocks),
            out_specs=(VMEM, VMEM),
            scratch_shapes=[pltpu.SemaphoreType.DMA((len(group),))],
            input_output_aliases={1: 0} if blocks else {},
            compiler_params=params(SCOPED),
            cost_estimate=cost(0, 2 * len(group) * width * step),
        )(weights, *(in_vmem(block) for block in blocks))

    blocks, done = load(groups[0], packed)
    if direct:
        parts = [packed] + [None] * (n_ep - 1)
        for bits in exchange_order(n_ep):
            parts[bits] = flip(packed, "ep", bits)
        parts = [following(part, done) for part in parts]
        stacked = pl.pallas_call(
            stack_kernel,
            out_shape=jax.ShapeDtypeStruct((n_ep, rows_here, width + LANES), jnp.bfloat16),
            in_specs=[VMEM] * n_ep,
            out_specs=VMEM,
            compiler_params=params(4),
        )(*parts)
        if len(groups) > 1:
            blocks, done = load(groups[1], stacked, blocks)
        parts = [stacked] + [following(shift(stacked, "dp", j), done) for j in range(1, n_dp)]
    else:
        for group in groups[1:]:
            blocks, done = load(group, done, blocks)
        parts = [lax.all_gather(packed, ("ep", "dp"), axis=0, tiled=True)[None]]

    x, own = pl.pallas_call(
        functools.partial(gather_kernel, pieces),
        out_shape=(
            pltpu.VMEM((rows, width + LANES), jnp.bfloat16),
            jax.ShapeDtypeStruct((share, piece), jnp.float32),
        ),
        in_specs=[VMEM] * (len(parts) + 1),
        out_specs=(VMEM, VMEM),
        scratch_shapes=[pltpu.VMEM((rows, width + LANES), jnp.float32)],
        compiler_params=params(SCOPED),
    )(in_vmem(blocks), *parts)

    units = pltpu.VMEM((n_parts, cols, part_width), jnp.bfloat16)
    hidden, gate, out, slots = pl.pallas_call(
        functools.partial(up_kernel, pieces),
        out_shape=(
            pltpu.VMEM((rows, cols), jnp.bfloat16),
            pltpu.VMEM((rows, LANES), jnp.float32),
            pltpu.VMEM((rows, piece), jnp.bfloat16),
            units,
        ),
        in_specs=[VMEM] * 2 + [ANY] * 2,
        out_specs=(VMEM,) * 4,
        scratch_shapes=[
            pltpu.VMEM((max(1, n_late), width, step), jnp.bfloat16),
            units,
            pltpu.SemaphoreType.DMA((max(1, n_late),)),
            pltpu.SemaphoreType.DMA((n_parts,)),
            pltpu.SemaphoreType.DMA((n_parts,)),
        ],
        compiler_params=params(SCOPED),
        cost_estimate=cost(2 * rows * cols * (width + piece), 24 * MIB),
    )(in_vmem(blocks), in_vmem(x), w_up, w_down)

    received = []
    gathering = [shift(out, "dp", plan[0][1])] if plan[0][1] else []
    after = out
    shared = dict(compiler_params=params(14), cost_estimate=cost(2 * rows * cols * piece, 2 * cols * piece))
    for stage in range(1, len(plan) - n_dp):
        jt, jd = plan[stage]
        loaded = n_parts
        out, slots = pl.pallas_call(
            functools.partial(down_kernel, pieces, stage),
            out_shape=(
                pltpu.VMEM((rows, piece), jnp.bfloat16 if jd else jnp.float32),
                pltpu.VMEM((loaded, cols, part_width), jnp.bfloat16),
            ),
            in_specs=[VMEM] * 3 + [ANY],
            out_specs=(VMEM,) * 2,
            scratch_shapes=[pltpu.SemaphoreType.DMA((loaded,))],
            **shared,
        )(in_vmem(hidden), in_vmem(gate), in_vmem(slots), following(w_down, after))
        if jd:
            gathering.append(shift(out, "dp", jd))
        else:
            after = pl.pallas_call(
                add_kernel,
                out_shape=jax.ShapeDtypeStruct((rows, piece), jnp.bfloat16),
                in_specs=[VMEM] * (1 + len(gathering)),
                out_specs=VMEM,
                compiler_params=params(4),
            )(out, *gathering)
            received.append(shift(after, "tp", jt))
            gathering = []
    *outs, out = pl.pallas_call(
        functools.partial(last_down_kernel, pieces),
        out_shape=tuple(
            pltpu.VMEM((rows, piece), jnp.bfloat16 if jd else jnp.float32) for jd in reversed(range(n_dp))
        ),
        in_specs=[VMEM] * 3 + [ANY],
        out_specs=(VMEM,) * n_dp,
        scratch_shapes=[
            pltpu.VMEM((n_dp * n_parts - slots.shape[0], cols, part_width), jnp.bfloat16),
            pltpu.SemaphoreType.DMA((n_dp * n_parts - slots.shape[0],)),
        ],
        **shared,
    )(in_vmem(hidden), in_vmem(gate), in_vmem(slots), following(w_down, after))
    gathering = [shift(x, "dp", plan[len(plan) - n_dp + j][1]) for j, x in enumerate(outs)]
    kept = pl.pallas_call(
        add_kernel,
        out_shape=jax.ShapeDtypeStruct((rows, piece), jnp.float32),
        in_specs=[VMEM] * (1 + len(received)),
        out_specs=VMEM,
        compiler_params=params(4),
    )(out, *received)
    arrived = [kept, *gathering]
    if direct:
        keep, *sends = pl.pallas_call(
            functools.partial(split_kernel, len(arrived)),
            out_shape=(
                jax.ShapeDtypeStruct((share, piece), jnp.float32),
                *(jax.ShapeDtypeStruct((share, piece), jnp.bfloat16) for _ in range(n_ep - 1)),
            ),
            in_specs=[VMEM] * len(arrived),
            out_specs=(VMEM,) * n_ep,
            compiler_params=params(4),
        )(*arrived)
        received = [flip(sends[bits - 1], "ep", bits) for bits in exchange_order(n_ep)]
    else:
        total = sum(x.astype(jnp.float32) for x in arrived)
        keep = lax.psum_scatter(total, "ep", scatter_dimension=0, tiled=True)
        received = []
    gain = norm_gain[None, :]
    scaled = pl.pallas_call(
        feature_kernel,
        out_shape=jax.ShapeDtypeStruct((share, piece), jnp.bfloat16),
        in_specs=[VMEM] * (3 + len(received)),
        out_specs=VMEM,
        compiler_params=params(4),
    )(keep, own, gain, *received)
    if direct:
        blocks = [scaled] + [None] * (n_ep - 1)
        for bits in exchange_order(n_ep):
            blocks[bits] = flip(scaled, "ep", bits)
        mine = pl.pallas_call(
            order_kernel,
            out_shape=jax.ShapeDtypeStruct((rows, piece), jnp.bfloat16),
            in_specs=[VMEM] * n_ep,
            out_specs=VMEM,
            compiler_params=params(4),
        )(*blocks)
    else:
        mine = lax.all_gather(scaled, "ep", axis=0, tiled=True)
    others = [shift(mine, "dp", j) for j in range(1, n_dp)]
    out_cols = w_qkv.shape[1]
    share = rows // n_tp
    first = pl.pallas_call(
        functools.partial(first_project_kernel, n_dp),
        out_shape=jax.ShapeDtypeStruct((rows, out_cols + LANES), jnp.float32),
        in_specs=[VMEM] * 3,
        out_specs=VMEM,
        compiler_params=params(12),
    )(mine, gain, w_qkv)
    projected = pl.pallas_call(
        functools.partial(project_kernel, pieces),
        out_shape=(
            jax.ShapeDtypeStruct((share, out_cols), jnp.float32),
            jax.ShapeDtypeStruct((share, LANES), jnp.float32),
            *(jax.ShapeDtypeStruct((share, out_cols + LANES), jnp.bfloat16) for _ in range(n_tp - 1)),
        ),
        in_specs=[VMEM] * (n_dp + 2),
        out_specs=tuple(VMEM for _ in range(n_tp + 1)),
        scratch_shapes=[pltpu.VMEM((rows, out_cols + LANES), jnp.float32)],
        compiler_params=params(12),
    )(*others, first, gain, w_qkv)
    total, squares = projected[0], projected[1]
    for j in range(1, n_tp):
        received = shift(projected[1 + j], "tp", j).astype(jnp.float32)
        total = total + received[:, :out_cols]
        squares = squares + received[:, out_cols:]
    scale = lax.rsqrt(jnp.sum(squares[:, :3], axis=1, keepdims=True) / width + EPSILON)
    return (total * scale).astype(jnp.bfloat16)


def solution(mesh):
    return jax.shard_map(
        body,
        mesh=mesh,
        in_specs=(
            P(("group", "ep", "dp"), None),
            P("tp"),
            P(("group", "ep", "dp"), None),
            P(("group", "ep", "dp"), None),
            P(None, ("ep", "tp", "dp")),
            P(("ep", "tp", "dp"), None),
            P("tp", ("ep", "dp")),
        ),
        out_specs=P(("group", "tp"), ("ep", "dp")),
        check_vma=False,
    )
```

```python
import functools

import jax
import jax.numpy as jnp
from jax import lax
from jax.experimental import pallas as pl
from jax.experimental.pallas import tpu as pltpu
from jax.sharding import PartitionSpec as P

FF = 6144
EXPERTS = 8
EPSILON = 1e-05
LANES = 128
MIB = 1 << 20


def expert_index(col_count):
    place = lax.axis_index("ep") * lax.axis_size("tp") + lax.axis_index("tp")
    place = place * lax.axis_size("dp") + lax.axis_index("dp")
    return place * col_count // FF


def pack_kernel(tokens_ref, ids_ref, weight_ref, out_ref, ids, weight, sem):
    rows, width = tokens_ref.shape
    copies = [
        pltpu.make_async_copy(ids_ref, ids, sem.at[0]),
        pltpu.make_async_copy(weight_ref, weight, sem.at[1]),
        *(
            pltpu.make_async_copy(
                tokens_ref.at[:, pl.ds(i * width // 4, width // 4)],
                out_ref.at[:, pl.ds(i * width // 4, width // 4)],
                sem.at[2 + i],
            )
            for i in range(4)
        ),
    ]
    for copy in copies:
        copy.start()
    copies[0].wait()
    copies[1].wait()
    gates = (weight[...] / jnp.sum(weight[...], axis=0, keepdims=True)).astype(jnp.bfloat16)
    gates = gates.astype(jnp.float32)
    row = lax.broadcasted_iota(jnp.int32, (rows, rows), 0)
    same = row == lax.broadcasted_iota(jnp.int32, (rows, rows), 1)
    column = lax.broadcasted_iota(jnp.int32, (rows, LANES), 1)
    spread = jnp.zeros((rows, LANES), jnp.float32)
    for k in range(ids.shape[0]):
        named = jnp.sum(jnp.where(same, ids[k : k + 1, :], 0), axis=1, keepdims=True)
        gate = jnp.sum(jnp.where(same, gates[k : k + 1, :], 0.0), axis=1, keepdims=True)
        spread += jnp.where(column == named, gate, 0.0)
    out_ref[:, width:] = spread.astype(jnp.bfloat16)
    for copy in copies[2:]:
        copy.wait()


def up_plan(cols):
    step = 1024 if cols % 1024 == 0 else cols
    count = cols // step
    early = max(1, count - 1)
    return step, early, count - early


def down_plan(width, pieces):
    n_tp, n_dp = pieces
    piece = width // (n_tp * n_dp)
    parts = max(1, -(-piece // 512))
    return piece, parts, [(jt, jd) for jt in reversed(range(n_tp)) for jd in reversed(range(n_dp))]


def own_place(pieces, jt=0, jd=0):
    n_tp, n_dp = pieces
    at_tp = lax.rem(lax.axis_index("tp") + jt, n_tp)
    at_dp = lax.rem(lax.axis_index("dp") + jd, n_dp)
    return at_tp * n_dp + at_dp


def load_kernel(w_up_ref, blocks_ref, done_ref, sem):
    count, _, step = blocks_ref.shape
    copies = [
        pltpu.make_async_copy(w_up_ref.at[:, pl.ds(b * step, step)], blocks_ref.at[b], sem.at[b])
        for b in range(count)
    ]
    for copy in copies:
        copy.start()
    for copy in copies:
        copy.wait()
    done_ref[...] = jnp.zeros_like(done_ref)


def stack_kernel(order, *refs):
    for bits, part in zip((0, *order), refs):
        refs[-1][bits] = part[...]


def gather_kernel(pieces, *refs):
    n_dp = pieces[1]
    parts, (x_ref, own_ref, wide) = refs[1:-3], refs[-3:]
    n_blocks, each, _ = parts[0].shape
    for j, part in enumerate(parts):
        from_dp = lax.rem(lax.axis_index("dp") + n_dp - j, n_dp)
        for e in range(n_blocks):
            if n_blocks == 1:
                at = 0
            else:
                at = pl.multiple_of(((lax.axis_index("ep") ^ e) * n_dp + from_dp) * each, each)
            wide[pl.ds(at, each), :] = part[e].astype(jnp.float32)
    x_ref[...] = wide[...].astype(jnp.bfloat16)
    share, piece = own_ref.shape
    own_ref[...] = wide[
        pl.ds(pl.multiple_of(lax.axis_index("ep") * share, share), share),
        pl.ds(pl.multiple_of(own_place(pieces) * piece, LANES), piece),
    ]


def down_copy(pieces, stage, part, w_down_ref, slot, sem):
    piece, parts, plan = down_plan(w_down_ref.shape[1], pieces)
    jt, jd = plan[stage]
    part_width = piece // parts
    start = pl.multiple_of(own_place(pieces, jt, jd) * piece + part * part_width, LANES)
    return pltpu.make_async_copy(w_down_ref.at[:, pl.ds(start, part_width)], slot, sem)


def up_kernel(pieces, blocks_ref, x_ref, *refs):
    w_up_ref, w_down_ref, hidden_ref, gate_ref, out_ref, next_ref, late, slots = refs[:8]
    late_sem, slot_sem, next_sem = refs[8:]
    width, cols = w_up_ref.shape
    rows = x_ref.shape[0]
    step, _, n_late = up_plan(cols)
    parts = slots.shape[0]
    early = blocks_ref.shape[0]

    def late_copy(b):
        start = pl.multiple_of((early + b) * step, step)
        return pltpu.make_async_copy(w_up_ref.at[:, pl.ds(start, step)], late.at[b], late_sem.at[b])

    @pl.loop(0, n_late)
    def _(b):
        late_copy(b).start()

    @pl.loop(0, parts)
    def _(part):
        down_copy(pieces, 0, part, w_down_ref, slots.at[part], slot_sem.at[part]).start()

    @pl.loop(0, parts)
    def _(part):
        down_copy(pieces, 1, part, w_down_ref, next_ref.at[part], next_sem.at[part]).start()

    def activate(b, block):
        up = jnp.dot(x_ref[:, :width], block, preferred_element_type=jnp.float32)
        at = pl.multiple_of(b * step, LANES if step % LANES == 0 else step)
        hidden_ref[:, pl.ds(at, step)] = (up / (1.0 + jnp.exp(-up))).astype(jnp.bfloat16)

    @pl.loop(0, early)
    def _(b):
        activate(b, blocks_ref[b])

    @pl.loop(0, n_late)
    def _(b):
        late_copy(b).wait()
        activate(early + b, late[b])

    mine = expert_index(cols)
    column = lax.broadcasted_iota(jnp.int32, (rows, LANES), 1)
    gate = jnp.sum(
        jnp.where(column == mine, x_ref[:, width:].astype(jnp.float32), 0.0), axis=1, keepdims=True
    )
    gate_ref[...] = jnp.broadcast_to(gate, gate_ref.shape)

    @pl.loop(0, parts)
    def _(part):
        down_copy(pieces, 0, part, w_down_ref, slots.at[part], slot_sem.at[part]).wait()
        work_part(part, hidden_ref, gate_ref, slots[part], out_ref)

    @pl.loop(0, parts)
    def _(part):
        down_copy(pieces, 1, part, w_down_ref, next_ref.at[part], next_sem.at[part]).wait()


def work_part(part, hidden_ref, gate_ref, block, out_ref):
    part_width = block.shape[1]
    value = jnp.dot(hidden_ref[...], block, preferred_element_type=jnp.float32) * gate_ref[:, :1]
    at = pl.multiple_of(part * part_width, LANES)
    out_ref[:, pl.ds(at, part_width)] = value.astype(out_ref.dtype)


def down_kernel(pieces, stage, hidden_ref, gate_ref, slots, w_down_ref, out_ref, next_ref, sem):
    @pl.loop(0, next_ref.shape[0])
    def _(part):
        down_copy(pieces, stage + 1, part, w_down_ref, next_ref.at[part], sem.at[part]).start()

    @pl.loop(0, slots.shape[0])
    def _(part):
        work_part(part, hidden_ref, gate_ref, slots[part], out_ref)

    @pl.loop(0, next_ref.shape[0])
    def _(part):
        down_copy(pieces, stage + 1, part, w_down_ref, next_ref.at[part], sem.at[part]).wait()


def last_down_kernel(pieces, hidden_ref, gate_ref, first_ref, w_down_ref, *refs):
    n_dp = pieces[1]
    outs, (slots, sem) = refs[:n_dp], refs[n_dp:]
    piece, parts, plan = down_plan(w_down_ref.shape[1], pieces)
    before = len(plan) - n_dp
    count, _, cut_width = slots.shape
    cuts = piece // cut_width

    def copy(j, cut):
        at = (j - 1) * cuts + cut
        jt, jd = plan[before + j]
        start = pl.multiple_of(own_place(pieces, jt, jd) * piece + cut * cut_width, LANES)
        return pltpu.make_async_copy(w_down_ref.at[:, pl.ds(start, cut_width)], slots.at[at], sem.at[at])

    for j in range(1, n_dp):

        @pl.loop(0, cuts)
        def _(cut, j=j):
            copy(j, cut).start()

    @pl.loop(0, parts)
    def _(part):
        work_part(part, hidden_ref, gate_ref, first_ref[part], outs[0])

    for j in range(1, n_dp):

        @pl.loop(0, cuts)
        def _(cut, j=j):
            copy(j, cut).wait()
            work_part(cut, hidden_ref, gate_ref, slots[(j - 1) * cuts + cut], outs[j])


def add_kernel(*refs):
    total = refs[0][...].astype(jnp.float32)
    for part in refs[1:-1]:
        total = total + part[...].astype(jnp.float32)
    refs[-1][...] = total.astype(refs[-1].dtype)


def split_kernel(n_in, *refs):
    parts, (keep_ref, *sends) = refs[:n_in], refs[n_in:]
    share = keep_ref.shape[0]
    for e in reversed(range(len(sends) + 1)):
        at = pl.ds(pl.multiple_of((lax.axis_index("ep") ^ e) * share, share), share)
        total = parts[0][at, :].astype(jnp.float32)
        for part in parts[1:]:
            total = total + part[at, :].astype(jnp.float32)
        if e:
            sends[e - 1][...] = total.astype(jnp.bfloat16)
        else:
            keep_ref[...] = total


def feature_kernel(keep_ref, own_ref, gain_ref, *refs):
    received, out_ref = refs[:-1], refs[-1]
    piece = out_ref.shape[1]
    total = keep_ref[...]
    for part in received:
        total = total + part[...].astype(jnp.float32)
    at = pl.ds(pl.multiple_of(lax.axis_index("dp") * piece, piece), piece)
    out_ref[...] = ((total + own_ref[...]) * gain_ref[:, at]).astype(jnp.bfloat16)


def order_kernel(order, *refs):
    blocks, out_ref = refs[:-1], refs[-1]
    share = blocks[0].shape[0]
    for bits, block in zip((0, *order), blocks):
        at = pl.multiple_of((lax.axis_index("ep") ^ bits) * share, share)
        out_ref[pl.ds(at, share), :] = block[...]


def project_piece(n_dp, j, x_ref, gain_ref, w_ref):
    piece = x_ref.shape[1]
    at = lax.rem(lax.axis_index("dp") + n_dp - j, n_dp)
    rows = pl.ds(pl.multiple_of(at * piece, piece), piece)
    x = x_ref[...]
    plain = x.astype(jnp.float32) * (1.0 / gain_ref[:, rows])
    product = jnp.dot(x, w_ref[rows, :], preferred_element_type=jnp.float32)
    return product, jnp.sum(plain * plain, axis=1, keepdims=True)


def first_project_kernel(n_dp, x_ref, gain_ref, w_ref, out_ref):
    cols = w_ref.shape[1]
    product, square = project_piece(n_dp, 0, x_ref, gain_ref, w_ref)
    out_ref[:, :cols] = product
    out_ref[:, cols:] = jnp.broadcast_to(square, (square.shape[0], LANES))


def project_kernel(pieces, *refs):
    n_tp, n_dp = pieces
    others, refs = refs[: n_dp - 1], refs[n_dp - 1 :]
    first_ref, gain_ref, w_ref, keep_ref, square_ref = refs[:5]
    sends, total_ref = refs[5:-1], refs[-1]
    cols = w_ref.shape[1]
    total = first_ref[:, :cols]
    square = first_ref[:, cols : cols + 1]
    for j, x_ref in enumerate(others):
        term, part = project_piece(n_dp, j + 1, x_ref, gain_ref, w_ref)
        total = total + term
        square = square + part
    high = square.astype(jnp.bfloat16).astype(jnp.float32)
    middle = (square - high).astype(jnp.bfloat16).astype(jnp.float32)
    low = square - high - middle
    lane = lax.broadcasted_iota(jnp.int32, (square.shape[0], LANES), 1)
    tail = jnp.where(lane == 0, high, jnp.where(lane == 1, middle, jnp.where(lane == 2, low, 0.0)))
    total_ref[:, :cols] = total
    total_ref[:, cols:] = tail
    share = keep_ref.shape[0]
    tp_index = lax.axis_index("tp")
    mine = pl.ds(pl.multiple_of(tp_index * share, share), share)
    keep_ref[...] = total_ref[mine, :cols]
    square_ref[...] = total_ref[mine, cols:]
    for j, send_ref in enumerate(sends):
        theirs = lax.rem(tp_index + j + 1, n_tp)
        send_ref[...] = total_ref[pl.ds(pl.multiple_of(theirs * share, share), share), :].astype(jnp.bfloat16)


def scale_kernel(width, keep_ref, square_ref, *refs):
    received, out_ref = refs[:-1], refs[-1]
    cols = out_ref.shape[1]
    total = keep_ref[...]
    squares = square_ref[...]
    for part in received:
        total = total + part[:, :cols].astype(jnp.float32)
        squares = squares + part[:, cols:].astype(jnp.float32)
    mean = jnp.sum(squares, axis=1, keepdims=True) / width
    out_ref[...] = (total * lax.rsqrt(mean + EPSILON)).astype(out_ref.dtype)


def shift(x, axis, by):
    size = lax.axis_size(axis)
    return lax.ppermute(x, axis, [(i, (i + by) % size) for i in range(size)])


def flip(x, axis, bits):
    size = lax.axis_size(axis)
    return lax.ppermute(x, axis, [(i, i ^ bits) for i in range(size)])


def exchange_order(n_ep):
    return sorted(range(1, n_ep), key=lambda bits: (bits < n_ep // 2, bits))


VMEM = pl.BlockSpec(memory_space=pltpu.VMEM)
ANY = pl.BlockSpec(memory_space=pl.ANY)
SCOPED = 24
SHARE = 1000


def params(mib):
    return pltpu.CompilerParams(vmem_limit_bytes=mib * MIB)


def cost(flops, bytes_accessed):
    return pl.CostEstimate(flops=flops // SHARE, transcendentals=0, bytes_accessed=bytes_accessed // SHARE)


def in_vmem(x):
    return pltpu.with_memory_space_constraint(x, pltpu.VMEM)


def body(tokens, norm_gain, expert_ids, route_weight, w_up, w_down, w_qkv):
    n_ep, n_tp, n_dp = (lax.axis_size(a) for a in ("ep", "tp", "dp"))
    rows_here, width = tokens.shape
    cols = w_up.shape[1]
    pieces = (n_tp, n_dp)
    rows = rows_here * n_ep * n_dp
    share = rows_here * n_dp
    step, early, n_late = up_plan(cols)
    piece, n_parts, plan = down_plan(width, pieces)
    part_width = piece // n_parts
    direct = n_ep <= 4

    packed = pl.pallas_call(
        pack_kernel,
        out_shape=jax.ShapeDtypeStruct((rows_here, width + LANES), jnp.bfloat16),
        in_specs=[ANY, ANY, ANY],
        out_specs=VMEM,
        scratch_shapes=[
            pltpu.VMEM(expert_ids.shape[::-1], jnp.int32),
            pltpu.VMEM(expert_ids.shape[::-1], jnp.float32),
            pltpu.SemaphoreType.DMA((6,)),
        ],
        compiler_params=params(2),
    )(*(pltpu.with_memory_space_constraint(x, pltpu.HBM) for x in (tokens, expert_ids.T, route_weight.T)))

    def following(x, after):
        return lax.optimization_barrier((x, after))[0]

    blocks, done = pl.pallas_call(
        load_kernel,
        out_shape=(
            pltpu.VMEM((early, width, step), jnp.bfloat16),
            jax.ShapeDtypeStruct((8, LANES), jnp.float32),
        ),
        in_specs=[ANY],
        out_specs=(VMEM, VMEM),
        scratch_shapes=[pltpu.SemaphoreType.DMA((early,))],
        compiler_params=params(SCOPED),
        cost_estimate=cost(0, 2 * early * width * step),
    )(following(w_up, packed))
    if direct:
        order = range(1, n_ep)
        parts = [packed] + [flip(packed, "ep", bits) for bits in order]
        parts = [following(part, done) for part in parts]
        stacked = pl.pallas_call(
            functools.partial(stack_kernel, order),
            out_shape=jax.ShapeDtypeStruct((n_ep, rows_here, width + LANES), jnp.bfloat16),
            in_specs=[VMEM] * n_ep,
            out_specs=VMEM,
            compiler_params=params(4),
        )(*parts)
        parts = [stacked] + [shift(stacked, "dp", j) for j in range(1, n_dp)]
    else:
        parts = [following(lax.all_gather(packed, ("ep", "dp"), axis=0, tiled=True), done)[None]]

    x, own = pl.pallas_call(
        functools.partial(gather_kernel, pieces),
        out_shape=(
            pltpu.VMEM((rows, width + LANES), jnp.bfloat16),
            jax.ShapeDtypeStruct((share, piece), jnp.float32),
        ),
        in_specs=[VMEM] * (len(parts) + 1),
        out_specs=(VMEM, VMEM),
        scratch_shapes=[pltpu.VMEM((rows, width + LANES), jnp.float32)],
        compiler_params=params(SCOPED),
    )(in_vmem(blocks), *parts)

    units = pltpu.VMEM((n_parts, cols, part_width), jnp.bfloat16)
    hidden, gate, out, slots = pl.pallas_call(
        functools.partial(up_kernel, pieces),
        out_shape=(
            pltpu.VMEM((rows, cols), jnp.bfloat16),
            pltpu.VMEM((rows, LANES), jnp.float32),
            pltpu.VMEM((rows, piece), jnp.bfloat16),
            units,
        ),
        in_specs=[VMEM] * 2 + [ANY] * 2,
        out_specs=(VMEM,) * 4,
        scratch_shapes=[
            pltpu.VMEM((max(1, n_late), width, step), jnp.bfloat16),
            units,
            pltpu.SemaphoreType.DMA((max(1, n_late),)),
            pltpu.SemaphoreType.DMA((n_parts,)),
            pltpu.SemaphoreType.DMA((n_parts,)),
        ],
        compiler_params=params(SCOPED),
        cost_estimate=cost(2 * rows * cols * (width + piece), 24 * MIB),
    )(in_vmem(blocks), in_vmem(x), w_up, w_down)

    received = []
    gathering = [shift(out, "dp", plan[0][1])] if plan[0][1] else []
    after = out
    shared = dict(compiler_params=params(14), cost_estimate=cost(2 * rows * cols * piece, 2 * cols * piece))
    for stage in range(1, len(plan) - n_dp):
        jt, jd = plan[stage]
        out, slots = pl.pallas_call(
            functools.partial(down_kernel, pieces, stage),
            out_shape=(
                pltpu.VMEM((rows, piece), jnp.bfloat16 if jd else jnp.float32),
                units,
            ),
            in_specs=[VMEM] * 3 + [ANY],
            out_specs=(VMEM,) * 2,
            scratch_shapes=[pltpu.SemaphoreType.DMA((n_parts,))],
            **shared,
        )(in_vmem(hidden), in_vmem(gate), in_vmem(slots), following(w_down, after))
        if jd:
            gathering.append(shift(out, "dp", jd))
        else:
            after = pl.pallas_call(
                add_kernel,
                out_shape=jax.ShapeDtypeStruct((rows, piece), jnp.bfloat16),
                in_specs=[VMEM] * (1 + len(gathering)),
                out_specs=VMEM,
                compiler_params=params(4),
            )(out, *gathering)
            received.append(shift(after, "tp", jt))
            gathering = []
    cut_width = part_width // 2 if part_width % (2 * LANES) == 0 else part_width
    n_cuts = max(1, n_dp - 1) * (piece // cut_width)
    *outs, out = pl.pallas_call(
        functools.partial(last_down_kernel, pieces),
        out_shape=tuple(
            pltpu.VMEM((rows, piece), jnp.bfloat16 if jd else jnp.float32) for jd in reversed(range(n_dp))
        ),
        in_specs=[VMEM] * 3 + [ANY],
        out_specs=(VMEM,) * n_dp,
        scratch_shapes=[
            pltpu.VMEM((n_cuts, cols, cut_width), jnp.bfloat16),
            pltpu.SemaphoreType.DMA((n_cuts,)),
        ],
        **shared,
    )(in_vmem(hidden), in_vmem(gate), in_vmem(slots), following(w_down, after))
    gathering = [shift(x, "dp", plan[len(plan) - n_dp + j][1]) for j, x in enumerate(outs)]
    kept = pl.pallas_call(
        add_kernel,
        out_shape=jax.ShapeDtypeStruct((rows, piece), jnp.float32),
        in_specs=[VMEM] * (1 + len(received)),
        out_specs=VMEM,
        compiler_params=params(4),
    )(out, *received)
    arrived = [kept, *gathering]
    if direct:
        keep, *sends = pl.pallas_call(
            functools.partial(split_kernel, len(arrived)),
            out_shape=(
                jax.ShapeDtypeStruct((share, piece), jnp.float32),
                *(jax.ShapeDtypeStruct((share, piece), jnp.bfloat16) for _ in range(n_ep - 1)),
            ),
            in_specs=[VMEM] * len(arrived),
            out_specs=(VMEM,) * n_ep,
            compiler_params=params(4),
        )(*arrived)
        received = [flip(sends[bits - 1], "ep", bits) for bits in exchange_order(n_ep)]
    else:
        total = sum(x.astype(jnp.float32) for x in arrived)
        keep = lax.psum_scatter(total, "ep", scatter_dimension=0, tiled=True)
        received = []
    gain = norm_gain[None, :]
    scaled = pl.pallas_call(
        feature_kernel,
        out_shape=jax.ShapeDtypeStruct((share, piece), jnp.bfloat16),
        in_specs=[VMEM] * (3 + len(received)),
        out_specs=VMEM,
        compiler_params=params(4),
    )(keep, own, gain, *received)
    if direct:
        order = range(1, n_ep)
        blocks = [scaled] + [flip(scaled, "ep", bits) for bits in order]
        mine = pl.pallas_call(
            functools.partial(order_kernel, order),
            out_shape=jax.ShapeDtypeStruct((rows, piece), jnp.bfloat16),
            in_specs=[VMEM] * n_ep,
            out_specs=VMEM,
            compiler_params=params(4),
        )(*blocks)
    else:
        mine = lax.all_gather(scaled, "ep", axis=0, tiled=True)
    others = [shift(mine, "dp", j) for j in range(1, n_dp)]
    out_cols = w_qkv.shape[1]
    share = rows // n_tp
    first = pl.pallas_call(
        functools.partial(first_project_kernel, n_dp),
        out_shape=jax.ShapeDtypeStruct((rows, out_cols + LANES), jnp.float32),
        in_specs=[VMEM] * 3,
        out_specs=VMEM,
        compiler_params=params(12),
    )(mine, gain, w_qkv)
    projected = pl.pallas_call(
        functools.partial(project_kernel, pieces),
        out_shape=(
            jax.ShapeDtypeStruct((share, out_cols), jnp.float32),
            jax.ShapeDtypeStruct((share, LANES), jnp.float32),
            *(jax.ShapeDtypeStruct((share, out_cols + LANES), jnp.bfloat16) for _ in range(n_tp - 1)),
        ),
        in_specs=[VMEM] * (n_dp + 2),
        out_specs=tuple(VMEM for _ in range(n_tp + 1)),
        scratch_shapes=[pltpu.VMEM((rows, out_cols + LANES), jnp.float32)],
        compiler_params=params(12),
    )(*others, first, gain, w_qkv)
    received = [shift(projected[1 + j], "tp", j) for j in range(1, n_tp)]
    return pl.pallas_call(
        functools.partial(scale_kernel, width),
        out_shape=jax.ShapeDtypeStruct((share, out_cols), jnp.bfloat16),
        in_specs=[VMEM] * (n_tp + 1),
        out_specs=VMEM,
        compiler_params=params(4),
    )(*projected[:2], *received)


def solution(mesh):
    return jax.shard_map(
        body,
        mesh=mesh,
        in_specs=(
            P(("group", "ep", "dp"), None),
            P("tp"),
            P(("group", "ep", "dp"), None),
            P(("group", "ep", "dp"), None),
            P(None, ("ep", "tp", "dp")),
            P(("ep", "tp", "dp"), None),
            P("tp", ("ep", "dp")),
        ),
        out_specs=P(("group", "tp"), ("ep", "dp")),
        check_vma=False,
    )
```
